32 devices in a mesh: req: 16 (over z, y, x), tp: 2 (over core).
Axes of the slice: x: 2, y: 2, z: 4, core: 2. Of those that a mesh axis runs over, the one named last changes fastest.
Arguments:
- queries: bfloat16 [4096, 2048], P('req', 'tp'), may hold values from -10 to 10
- new_kv: bfloat16 [4096, 2048], P('req', 'tp'), may hold values from -4 to 4
- kv_pool: bfloat16 [128, 4, 256, 2048], P('req', None, None, 'tp'), may hold values from -4 to 4
- cache_lens: int32 [128], P('req'), may hold values from 2 to 1024, as said below
- parents: int32 [128, 32], P('req'), may hold values from 0 to 31, as said below
- accepted: int32 [128], P('req'), may hold values from 0 to 31, as said below
- residual: bfloat16 [4096, 4096], P(('req', 'tp')), may hold values from -3 to 3
- w_out: bfloat16 [2048, 4096], P('tp'), may hold values from -0.125 to 0.125
- norm_gain: float32 [4096], replicated, may hold values from 0.25 to 1.75
Outputs:
- hidden_out: bfloat16 [4096, 4096], P(('req', 'tp'))
- normed: bfloat16 [4096, 4096], P(('req', 'tp'))
- accepted_kv: bfloat16 [128, 8, 2048], P('req', None, 'tp')
The draws below stay inside these ranges and needn't reach their ends.
Inputs may be any that keep to these rules, and one draw needn't show every extreme that they name: parents[r, 0] = 0 and parents[r, i] < i for i >= 1; every node lies at depth 7 or less; nodes 1 to 7 form a chain below the root. Some request's accepted node lies at depth 7. `cache_lens`: some request holds 1024 cached rows and some holds 2.
All inputs are finite; a program needn't handle non-finite values.
Results may differ from the reference program's by a relative error of at most 0.015.
Values may be sent and summed in bfloat16 or wider, within the bound.
A program may use at most 128 MiB of HBM per device.

```python
from functools import reduce
import jax
import jax.numpy as jnp
from jax import lax

D = 4096
HEADS = 16
KVH = 8
HD = 128
TREE = 32
MAXD = 7
PAGE = 256
PAGES = 4
REQ_DEV = 8
PATH = 8
REQUESTS = 128
TOKENS = 4096
N_REQ = 16
N_TP = 2


def draw_queries(key, part):
    first_key = jax.random.fold_in(jax.random.fold_in(key, 11), 0)
    values = jnp.clip(2.5 * jax.random.normal(first_key, (TOKENS, HEADS * HD), jnp.float32), -10.0, 10.0)
    return values.astype(jnp.bfloat16)


def draw_kv_pool(key, part):
    shape = (REQUESTS, PAGES, PAGE, KVH * 2 * HD)
    pool_key = jax.random.fold_in(key, 21)
    values = jnp.clip(jax.random.normal(pool_key, shape, jnp.float32), -4.0, 4.0)
    return values.astype(jnp.bfloat16)


def draw_cache_lens(key, part):
    first_key, second_key, third_key, fourth_key = jax.random.split(jax.random.fold_in(key, 31), 4)
    lowest = PAGE * (PAGES - 1) // 2 + 2
    long_lengths = jax.random.randint(first_key, (REQUESTS,), lowest, PAGES * PAGE + 1)
    short_lengths = jax.random.randint(second_key, (REQUESTS,), 2, PAGE + 1)
    is_short = jax.random.randint(third_key, (REQUESTS,), 0, 16) == 0
    lengths = jnp.where(is_short, short_lengths, long_lengths)
    longest = jax.random.randint(fourth_key, (), 0, REQUESTS)
    shortest = (longest + REQUESTS // 2) % REQUESTS
    request_ids = jnp.arange(REQUESTS, dtype=jnp.int32)
    lengths = jnp.where(request_ids == shortest, 2, lengths)
    return jnp.where(request_ids == longest, PAGES * PAGE, lengths).astype(jnp.int32)


def draw_parents(key, part):

    def one_tree(tree_key):

        def add_node(node, carry):
            parent_ids, depths = carry
            picked = jax.random.randint(jax.random.fold_in(tree_key, node), (), 0, node)
            picked = jnp.where(node <= MAXD, node - 1, picked)
            picked = jnp.where(depths[picked] >= MAXD, parent_ids[picked], picked)
            parent_ids = parent_ids.at[node].set(picked)
            depths = depths.at[node].set(depths[picked] + 1)
            return (parent_ids, depths)
        start_ids = jnp.zeros((TREE,), jnp.int32)
        parent_ids, depths = lax.fori_loop(1, TREE, add_node, (start_ids, start_ids))
        return parent_ids
    tree_keys = jax.random.split(jax.random.fold_in(key, 41), REQUESTS)
    return jax.vmap(one_tree)(tree_keys).astype(jnp.int32)


def draw_accepted(key, part):
    first_key, second_key = jax.random.split(jax.random.fold_in(key, 51), 2)
    nodes_drawn = jax.random.randint(first_key, (REQUESTS,), 0, TREE)
    deepest = jax.random.randint(second_key, (), 0, REQUESTS)
    return jnp.where(jnp.arange(REQUESTS, dtype=jnp.int32) == deepest, MAXD, nodes_drawn).astype(jnp.int32)


def shard_levels(stream_key, dims, cuts, smallest, top_value):
    gain, own = 1.0, jax.random.fold_in(stream_key, 6)
    for position, shards_of in cuts:
        draws = jnp.exp(jax.random.uniform(jax.random.fold_in(own, position), (shards_of,), jnp.float32, smallest / len(cuts), top_value / len(cuts)))
        gain = gain * jnp.repeat(draws, dims[position] // shards_of).reshape([-1 if axis == position else 1 for axis in range(len(dims))])
    return gain


def gaussian(own_key, dims, spread, bound, shards=(), kind=jnp.bfloat16):
    drawn = jax.random.normal(own_key, dims, jnp.float32) * spread
    if len(shards) > 0:
        drawn = shard_levels(own_key, dims, shards, -0.22, 0.18) * drawn
    return jnp.clip(drawn, min=-bound, max=bound).astype(kind)


def setup_inputs(seed: int = 0) -> dict:
    arg_keys = jax.random.split(jax.random.key(seed), 10)
    return {
        "queries": draw_queries(jax.random.fold_in(arg_keys[9], 71), 0),
        "new_kv": gaussian(arg_keys[1], (TOKENS, KVH * 2 * HD), 1.0, 4.0, ((0, 16), (1, 2))),
        "kv_pool": draw_kv_pool(jax.random.fold_in(arg_keys[9], 71), 0),
        "cache_lens": draw_cache_lens(jax.random.fold_in(arg_keys[9], 71), 0),
        "parents": draw_parents(jax.random.fold_in(arg_keys[9], 71), 0),
        "accepted": draw_accepted(jax.random.fold_in(arg_keys[9], 71), 0),
        "residual": gaussian(arg_keys[6], (TOKENS, D), 0.5, 3.0, ((0, 32),)),
        "w_out": gaussian(arg_keys[7], (HEADS * HD, D), (HEADS * HD) ** -0.5, 0.125, ((0, 2),)),
        "norm_gain": jnp.clip(1.0 + 0.15 * jax.random.normal(arg_keys[8], (D,), jnp.float32), 0.25, 1.75),
    }


NEGATIVE = -1e+30

def ancestors(parents):
    node_ids = jnp.arange(TREE, dtype=jnp.int32)
    current = jnp.broadcast_to(node_ids, parents.shape)
    marked = jnp.zeros(parents.shape + (TREE,), jnp.int32)
    for depth_step in range(MAXD + 1):
        onehot_rows = (current[..., None] == node_ids).astype(jnp.int32)
        marked = jnp.maximum(marked, onehot_rows)
        current = lax.optimization_barrier(jnp.sum(onehot_rows * parents[..., None, :], axis=-1, dtype=jnp.int32))
    return marked

def block_partial(query_rows, key_rows, value_rows, allowed):
    scale_factor = HD ** (-0.5)
    scores = jnp.einsum('tkgd,ckd->tkgc', query_rows, key_rows) * scale_factor
    visible = allowed[:, None, None, :]
    largest = lax.optimization_barrier(jnp.max(jnp.where(visible, scores, NEGATIVE), axis=-1))
    weights = jnp.where(visible, jnp.exp(scores - largest[..., None]), 0.0)
    totals = lax.optimization_barrier(jnp.sum(weights, axis=-1))
    rounded = lax.optimization_barrier(weights.astype(jnp.bfloat16)).astype(jnp.float32)
    weighted = jnp.einsum('tkgc,ckd->tkgd', rounded, value_rows)
    return (largest, totals, weighted)

def merge_blocks(block_list):
    largest = reduce(jnp.maximum, [block_part[0] for block_part in block_list])
    factors = [jnp.exp(block_part[0] - largest) for block_part in block_list]
    denominator = reduce(jnp.add, [factor * block_part[1] for factor, block_part in zip(factors, block_list)])
    numerator = reduce(jnp.add, [factor[..., None] * block_part[2] for factor, block_part in zip(factors, block_list)])
    return (denominator, numerator)

def reference(queries, new_kv, kv_pool, cache_lens, parents, accepted, residual, w_out, norm_gain):
    group = HEADS // KVH
    row_width = KVH * 2 * HD
    marked_all = ancestors(parents)

    def attend(request):
        first_row = request * TREE
        query_rows = lax.dynamic_slice_in_dim(queries, first_row, TREE, 0).astype(jnp.float32).reshape(TREE, KVH, group, HD)
        fresh = lax.dynamic_slice_in_dim(new_kv, first_row, TREE, 0).astype(jnp.float32).reshape(TREE, KVH, 2, HD)
        length = cache_lens[request]
        marked = marked_all[request]
        block_list = [block_partial(query_rows, fresh[:, :, 0], fresh[:, :, 1], marked > 0)]
        home = request // REQ_DEV
        within = request % REQ_DEV
        for page_index in range(PAGES):
            holder = ((home + page_index) % N_REQ * REQ_DEV + within).astype(jnp.int32)
            page_rows = lax.dynamic_slice(kv_pool, (holder, jnp.int32(page_index), jnp.int32(0), jnp.int32(0)), (1, 1, PAGE, row_width))
            page_rows = page_rows.reshape(PAGE, KVH, 2, HD).astype(jnp.float32)
            positions = page_index * PAGE + jnp.arange(PAGE, dtype=jnp.int32)
            allowed = jnp.broadcast_to((positions < length)[None, :], (TREE, PAGE))
            block_list.append(block_partial(query_rows, page_rows[:, :, 0], page_rows[:, :, 1], allowed))
        denominator, numerator = merge_blocks(block_list)
        return (numerator / denominator[..., None]).reshape(TREE, HEADS * HD).astype(jnp.bfloat16)
    attention = lax.map(attend, jnp.arange(REQUESTS, dtype=jnp.int32)).reshape(TOKENS, HEADS * HD)
    group_width = HEADS * HD // N_TP
    summed = jnp.zeros((TOKENS, D), jnp.float32)
    for group_index in range(N_TP):
        low = group_index * group_width
        product = jnp.dot(attention[:, low:low + group_width], w_out[low:low + group_width], preferred_element_type=jnp.float32)
        summed = summed + lax.optimization_barrier(product.astype(jnp.bfloat16)).astype(jnp.float32)
    hidden_out = (residual.astype(jnp.float32) + summed).astype(jnp.bfloat16)
    widened = hidden_out.astype(jnp.float32)
    normed = (widened * lax.rsqrt(lax.optimization_barrier(jnp.mean(widened * widened, axis=-1, keepdims=True)) + 1e-05) * norm_gain).astype(jnp.bfloat16)
    node_ids = jnp.arange(TREE, dtype=jnp.int32)
    chosen = (accepted[:, None] == node_ids[None, :]).astype(jnp.int32)
    on_path = lax.optimization_barrier(jnp.sum(chosen[:, :, None] * marked_all, axis=1, dtype=jnp.int32))
    path_rank = jnp.cumsum(on_path, axis=1, dtype=jnp.int32) - 1
    path_slots = jnp.arange(PATH, dtype=jnp.int32)
    selector = ((path_rank[:, None, :] == path_slots[None, :, None]) & (on_path[:, None, :] > 0)).astype(jnp.float32)
    fresh_rows = new_kv.reshape(REQUESTS, TREE, row_width).astype(jnp.float32)
    accepted_kv = jnp.einsum('rku,ruc->rkc', selector, fresh_rows).astype(jnp.bfloat16)
    return (hidden_out, normed, accepted_kv)
```

```python
import functools

import jax
import jax.numpy as jnp
from jax import lax
from jax.experimental import pallas as pl
from jax.experimental.pallas import tpu as pltpu
from jax.sharding import PartitionSpec as P

HD = 128
TREE = 32
PATH = 8
LANES = 128
NEGATIVE = -1e30
FLOOR = -1e29
SCALE2 = HD**-0.5 * 1.4426950408889634
MESH = pl.DeviceIdType.MESH
F32 = jnp.float32
BF16 = jnp.bfloat16


def iota(shape, axis):
    return lax.broadcasted_iota(jnp.int32, shape, axis)


def dot(left, right):
    return jnp.dot(left, right, preferred_element_type=F32)


def dot_t(left, right):
    return lax.dot_general(left, right, (((1,), (1,)), ((), ())), preferred_element_type=F32)


def indicator(mask, dtype=BF16):
    return jnp.where(mask, 1.0, 0.0).astype(dtype)


def tree_masks(parents, tokens):
    requests = tokens // TREE
    expand = indicator((iota((tokens, requests), 0) >> 5) == iota((tokens, requests), 1), F32)
    spread = dot(expand, parents.astype(F32))
    pick = (iota((tokens, TREE), 0) & (TREE - 1)) == iota((tokens, TREE), 1)
    parent = jnp.sum(jnp.where(pick, spread, 0.0), axis=1, keepdims=True)
    rows, columns = iota((tokens, tokens), 0), iota((tokens, tokens), 1)
    base = (rows & ~(TREE - 1)).astype(F32)
    one = indicator(columns.astype(F32) == parent + base, F32)
    eye = indicator(rows == columns, F32)
    two = dot(one.astype(BF16), one.astype(BF16))
    four = dot(two.astype(BF16), two.astype(BF16))
    reach = dot((eye + one).astype(BF16), (eye + two).astype(BF16))
    reach = dot(reach.astype(BF16), (eye + four).astype(BF16))
    return indicator(reach > 0.0)


def kernel(
    n_req, n_tp, chunk,
    lens_s, accepted_s, parents_ref, q_ref, fresh_ref, kv_hbm, residual_hbm, w_hbm, gain_ref,
    hidden_ref, normed_ref, path_ref,
    kv, w, residual, q_in, lens_own, lens_in, out_send, out_in, lse_send, lse_in,
    local_out, local_lse, lse_tile, tree, attention, own, proj_send, proj_in,
    load_sem, lens_send_sem, lens_recv_sem, q_send_sem, q_recv_sem, o_send_sem, o_recv_sem,
    l_send_sem, l_recv_sem, p_send_sem, p_recv_sem,
):
    me, tp = lax.axis_index("req"), lax.axis_index("tp")
    tokens, width = q_ref.shape
    requests = tokens // TREE
    heads = width // HD
    kv_heads = fresh_ref.shape[1] // (2 * HD)
    pages, page = kv.shape[0], kv.shape[2]
    part = tokens // n_tp
    per_part = part // chunk
    chunks = tokens // chunk
    features = w.shape[1]
    group = heads // kv_heads

    loads = [
        pltpu.make_async_copy(kv_hbm.at[:, p], kv.at[p], load_sem.at[p]) for p in range(pages)
    ]
    loads.append(pltpu.make_async_copy(w_hbm, w, load_sem.at[pages]))
    loads.append(pltpu.make_async_copy(residual_hbm, residual, load_sem.at[pages + 1]))
    for load in loads:
        load.start()

    def ahead(p):
        return lax.rem(me + p, n_req)

    def behind(p):
        return lax.rem(me + n_req - p, n_req)

    barrier = pltpu.get_barrier_semaphore()
    for p in range(1, pages):
        for other in (ahead(p), behind(p)):
            pl.semaphore_signal(barrier, inc=1, device_id={"req": other}, device_id_type=MESH)
    for j in range(1, n_tp):
        pl.semaphore_signal(
            barrier, inc=1, device_id={"tp": lax.rem(tp + j, n_tp)}, device_id_type=MESH
        )

    lens = jnp.zeros((requests, LANES), jnp.int32)
    for r in range(requests):
        lens = jnp.where(iota((requests, LANES), 0) == r, lens_s[r], lens)
    lens_own[...] = lens
    pl.semaphore_wait(barrier, 2 * (pages - 1) + n_tp - 1)

    def first_row(c):
        block = lax.rem(tp + 1 + c // per_part, n_tp)
        return pl.multiple_of(block * part + lax.rem(c, per_part) * chunk, chunk)

    def send_lens(p):
        return pltpu.make_async_remote_copy(
            lens_own, lens_in.at[p - 1], lens_send_sem.at[p - 1], lens_recv_sem.at[p - 1],
            device_id={"req": ahead(p)}, device_id_type=MESH,
        )

    def send_q(p, c):
        rows = pl.ds(first_row(c), chunk)
        return pltpu.make_async_remote_copy(
            q_ref.at[rows], q_in.at[p - 1, rows], q_send_sem.at[p - 1, c], q_recv_sem.at[p - 1, c],
            device_id={"req": ahead(p)}, device_id_type=MESH,
        )

    def send_out(p, c):
        rows = pl.ds(first_row(c), chunk)
        return pltpu.make_async_remote_copy(
            out_send.at[p - 1, rows], out_in.at[p - 1, rows],
            o_send_sem.at[p - 1, c], o_recv_sem.at[p - 1, c],
            device_id={"req": behind(p)}, device_id_type=MESH,
        )

    def send_lse(p, c):
        return pltpu.make_async_remote_copy(
            lse_send.at[p - 1, c], lse_in.at[p - 1, c],
            l_send_sem.at[p - 1, c], l_recv_sem.at[p - 1, c],
            device_id={"req": behind(p)}, device_id_type=MESH,
        )

    def send_proj(j):
        return pltpu.make_async_remote_copy(
            proj_send.at[j], proj_in.at[j], p_send_sem.at[j], p_recv_sem.at[j],
            device_id={"tp": lax.rem(tp + 1 + j, n_tp)}, device_id_type=MESH,
        )

    for p in range(1, pages):
        send_lens(p).start()

    @pl.loop(0, chunks)
    def _(c):
        for p in range(1, pages):
            send_q(p, c).start()

    marked = tree_masks(parents_ref[...], tokens)
    fold = indicator((iota((tokens, TREE), 0) & (TREE - 1)) == iota((tokens, TREE), 1))
    tree[...] = dot(marked, fold)
    accepted = jnp.zeros((requests, tokens), jnp.int32)
    for r in range(requests):
        accepted = jnp.where(iota((requests, tokens), 0) == r, accepted_s[r] + r * TREE, accepted)
    chosen = indicator(iota((requests, tokens), 1) == accepted, F32)
    on_path = dot(chosen, marked.astype(F32))
    upto = indicator(iota((tokens, tokens), 0) <= iota((tokens, tokens), 1), F32)
    count = dot(on_path, upto)
    slots = (requests * PATH, requests)
    spread = indicator((iota(slots, 0) >> 3) == iota(slots, 1), F32)
    slot = (iota((requests * PATH, tokens), 0) & (PATH - 1)).astype(F32) + 1.0
    selector = (dot(spread, count) == slot) & (dot(spread, on_path) > 0.0)
    path_ref[...] = dot(indicator(selector), fresh_ref[...]).astype(BF16)

    lane = iota((TREE, LANES), 1)

    def stacked_queries(ref, rows, k):
        columns = [slice((k * group + g) * HD, (k * group + g + 1) * HD) for g in range(group)]
        return jnp.concatenate([ref[rows, c] for c in columns], axis=0)

    def lens_mask(row, p):
        wide = jnp.concatenate([row] * (page // LANES), axis=1)
        return iota((1, page), 1) + p * page < wide

    loads[0].wait()

    @pl.loop(0, requests)
    def _(r):
        rows = pl.ds(pl.multiple_of(r * TREE, TREE), TREE)
        valid = lens_mask(lens_own[pl.ds(r, 1), :], 0)
        allowed = jnp.concatenate([tree[rows, :]] * group, axis=0) > 0.0
        lse = jnp.zeros((TREE, LANES), F32)
        for k in range(kv_heads):
            keys = slice(2 * k * HD, (2 * k + 1) * HD)
            values = slice((2 * k + 1) * HD, (2 * k + 2) * HD)
            query = stacked_queries(q_ref, rows, k)
            cached = jnp.where(valid, dot_t(query, kv[0, r, :, keys]) * SCALE2, NEGATIVE)
            drafted = jnp.where(allowed, dot_t(query, fresh_ref[rows, keys]) * SCALE2, NEGATIVE)
            largest = jnp.maximum(
                jnp.max(cached, axis=1, keepdims=True), jnp.max(drafted, axis=1, keepdims=True)
            )
            cached = jnp.exp2(cached - largest)
            drafted = jnp.exp2(drafted - largest)
            total = jnp.sum(cached, axis=1, keepdims=True) + jnp.sum(drafted, axis=1, keepdims=True)
            out = dot(cached.astype(BF16), kv[0, r, :, values])
            out = out + dot(drafted.astype(BF16), fresh_ref[rows, values])
            out = out / total
            level = largest + jnp.log2(total)
            for g in range(group):
                h = k * group + g
                some = slice(g * TREE, (g + 1) * TREE)
                local_out[rows, h * HD : (h + 1) * HD] = out[some]
                lse = jnp.where(lane == h, level[some], lse)
        local_lse[rows, :] = lse

    for p in range(1, pages):
        loads[p].wait()
        send_lens(p).wait_recv()

    @pl.loop(0, chunks)
    def _(c):
        start = first_row(c)
        for p in range(1, pages):
            send_q(p, c).wait_recv()

            @pl.loop(0, chunk // TREE)
            def _(i):
                r = start // TREE + i
                rows = pl.ds(pl.multiple_of(start + i * TREE, TREE), TREE)
                valid = lens_mask(lens_in[p - 1, pl.ds(r, 1), :], p)
                lse = jnp.zeros((TREE, LANES), F32)
                for k in range(kv_heads):
                    keys = slice(2 * k * HD, (2 * k + 1) * HD)
                    values = slice((2 * k + 1) * HD, (2 * k + 2) * HD)
                    query = stacked_queries(q_in.at[p - 1], rows, k)
                    cached = jnp.where(valid, dot_t(query, kv[p, r, :, keys]) * SCALE2, NEGATIVE)
                    largest = jnp.max(cached, axis=1, keepdims=True)
                    cached = jnp.exp2(cached - jnp.maximum(largest, FLOOR))
                    total = jnp.sum(cached, axis=1, keepdims=True)
                    out = dot(cached.astype(BF16), kv[p, r, :, values])
                    some_valid = total > 0.0
                    safe = jnp.where(some_valid, total, 1.0)
                    out = out / safe
                    level = jnp.where(some_valid, largest + jnp.log2(safe), NEGATIVE)
                    for g in range(group):
                        h = k * group + g
                        some = slice(g * TREE, (g + 1) * TREE)
                        out_send[p - 1, rows, h * HD : (h + 1) * HD] = out[some].astype(BF16)
                        lse = jnp.where(lane == h, level[some], lse)
                lse_tile[pl.ds(pl.multiple_of(i * TREE, TREE), TREE), :] = lse

            lse_send[p - 1, c] = lse_tile[...].T[:8]
            send_lse(p, c).start()
            send_out(p, c).start()

    loads[pages].wait()
    loads[pages + 1].wait()

    for j in range(n_tp):

        @pl.loop(0, per_part)
        def _(i):
            c = j * per_part + i
            rows = pl.ds(first_row(c), chunk)
            here = pl.ds(pl.multiple_of(i * chunk, chunk), chunk)
            levels = [local_lse[rows, :]]
            for p in range(1, pages):
                send_lse(p, c).wait_recv()
                send_out(p, c).wait_recv()
                tile = jnp.concatenate(
                    [lse_in[p - 1, c], jnp.zeros((LANES - 8, LANES), F32)], axis=0
                )
                levels.append(tile.T[:chunk])
            largest = functools.reduce(jnp.maximum, levels)
            factors = [jnp.exp2(level - largest) for level in levels]
            inverse = 1.0 / functools.reduce(jnp.add, factors)
            factors = [factor * inverse for factor in factors]
            for h in range(heads):
                columns = slice(h * HD, (h + 1) * HD)
                total = factors[0][:, h : h + 1] * local_out[rows, columns]
                for p in range(1, pages):
                    term = out_in[p - 1, rows, columns].astype(F32)
                    total = total + factors[p][:, h : h + 1] * term
                attention[here, columns] = total.astype(BF16)

        target = proj_send.at[j] if j < n_tp - 1 else own
        tile_width = min(features, 1024)

        @pl.loop(0, features // tile_width)
        def _(t):
            columns = pl.ds(pl.multiple_of(t * tile_width, tile_width), tile_width)
            target[:, columns] = dot(attention[...], w[:, columns]).astype(BF16)

        if j < n_tp - 1:
            send_proj(j).start()

    for j in range(n_tp - 1):
        send_proj(j).wait_recv()

    @pl.loop(0, part // 16)
    def _(i):
        rows = pl.ds(pl.multiple_of(i * 16, 16), 16)
        summed = own[rows, :].astype(F32)
        for j in range(n_tp - 1):
            summed = summed + proj_in[j, rows, :].astype(F32)
        hidden = (residual[rows, :].astype(F32) + summed).astype(BF16)
        hidden_ref[rows, :] = hidden
        wide = hidden.astype(F32)
        mean = jnp.sum(wide * wide, axis=1, keepdims=True) * (1.0 / features)
        normed_ref[rows, :] = (wide * lax.rsqrt(mean + 1e-05) * gain_ref[...]).astype(BF16)

    for p in range(1, pages):
        send_lens(p).wait_send()

    @pl.loop(0, chunks)
    def _(c):
        for p in range(1, pages):
            send_q(p, c).wait_send()
            send_lse(p, c).wait_send()
            send_out(p, c).wait_send()

    for j in range(n_tp - 1):
        send_proj(j).wait_send()


def per_device(n_req, n_tp, queries, new_kv, kv_pool, cache_lens, parents, accepted, residual, w_out, norm_gain):
    requests, pages, page, row_width = kv_pool.shape
    tokens, width = queries.shape
    features = w_out.shape[1]
    part = tokens // n_tp
    chunk = min(part, 2 * TREE)
    chunks = tokens // chunk
    away = pages - 1
    vmem = pl.BlockSpec(memory_space=pltpu.VMEM)
    smem = pl.BlockSpec(memory_space=pltpu.SMEM)
    hbm = pl.BlockSpec(memory_space=pl.ANY)
    dma = pltpu.SemaphoreType.DMA
    hidden_out, normed, path = pl.pallas_call(
        functools.partial(kernel, n_req, n_tp, chunk),
        out_shape=(
            jax.ShapeDtypeStruct((part, features), BF16),
            jax.ShapeDtypeStruct((part, features), BF16),
            jax.ShapeDtypeStruct((requests * PATH, row_width), BF16),
        ),
        in_specs=[smem, smem, vmem, vmem, vmem, hbm, hbm, hbm, vmem],
        out_specs=(vmem, vmem, vmem),
        scratch_shapes=[
            pltpu.VMEM((pages, requests, page, row_width), BF16),
            pltpu.VMEM(w_out.shape, BF16),
            pltpu.VMEM((part, features), BF16),
            pltpu.VMEM((away, tokens, width), BF16),
            pltpu.VMEM((requests, LANES), jnp.int32),
            pltpu.VMEM((away, requests, LANES), jnp.int32),
            pltpu.VMEM((away, tokens, width), BF16),
            pltpu.VMEM((away, tokens, width), BF16),
            pltpu.VMEM((away, chunks, 8, LANES), F32),
            pltpu.VMEM((away, chunks, 8, LANES), F32),
            pltpu.VMEM((tokens, width), F32),
            pltpu.VMEM((tokens, LANES), F32),
            pltpu.VMEM((LANES, LANES), F32),
            pltpu.VMEM((tokens, TREE), F32),
            pltpu.VMEM((part, width), BF16),
            pltpu.VMEM((part, features), BF16),
            pltpu.VMEM((max(n_tp - 1, 1), part, features), BF16),
            pltpu.VMEM((max(n_tp - 1, 1), part, features), BF16),
            dma((pages + 2,)),
            dma((away,)),
            dma((away,)),
            dma((away, chunks)),
            dma((away, chunks)),
            dma((away, chunks)),
            dma((away, chunks)),
            dma((away, chunks)),
            dma((away, chunks)),
            dma((max(n_tp - 1, 1),)),
            dma((max(n_tp - 1, 1),)),
        ],
        compiler_params=pltpu.CompilerParams(
            collective_id=0, has_side_effects=True, vmem_limit_bytes=56 * 2**20
        ),
    )(
        cache_lens, accepted, parents, queries, new_kv, kv_pool, residual, w_out,
        norm_gain.reshape(1, features),
    )
    return hidden_out, normed, path.reshape(requests, PATH, row_width)


def solution(mesh):
    placed = (
        P("req", "tp"),
        P("req", "tp"),
        P("req", None, None, "tp"),
        P("req"),
        P("req", None),
        P("req"),
        P(("req", "tp"), None),
        P("tp", None),
        P(),
    )
    return jax.shard_map(
        functools.partial(per_device, mesh.shape["req"], mesh.shape["tp"]),
        mesh=mesh,
        in_specs=placed,
        out_specs=(P(("req", "tp"), None), P(("req", "tp"), None), P("req", None, "tp")),
        check_vma=False,
    )
```

```python
import functools

import jax
import jax.numpy as jnp
from jax import lax
from jax.experimental import pallas as pl
from jax.experimental.pallas import tpu as pltpu
from jax.sharding import PartitionSpec as P

HD = 128
TREE = 32
PATH = 8
LANES = 128
NEGATIVE = -1e30
FLOOR = -1e29
SCALE2 = HD**-0.5 * 1.4426950408889634
MESH = pl.DeviceIdType.MESH
F32 = jnp.float32
BF16 = jnp.bfloat16


def iota(shape, axis):
    return lax.broadcasted_iota(jnp.int32, shape, axis)


def dot(left, right):
    return jnp.dot(left, right, preferred_element_type=F32)


def dot_t(left, right):
    return lax.dot_general(left, right, (((1,), (1,)), ((), ())), preferred_element_type=F32)


def indicator(mask, dtype=BF16):
    return jnp.where(mask, 1.0, 0.0).astype(dtype)


def tree_masks(parents, tokens):
    requests = tokens // TREE
    expand = indicator((iota((tokens, requests), 0) >> 5) == iota((tokens, requests), 1), F32)
    spread = dot(expand, parents.astype(F32))
    pick = (iota((tokens, TREE), 0) & (TREE - 1)) == iota((tokens, TREE), 1)
    parent = jnp.sum(jnp.where(pick, spread, 0.0), axis=1, keepdims=True)
    rows, columns = iota((tokens, tokens), 0), iota((tokens, tokens), 1)
    base = (rows & ~(TREE - 1)).astype(F32)
    one = indicator(columns.astype(F32) == parent + base, F32)
    eye = indicator(rows == columns, F32)
    two = dot(one.astype(BF16), one.astype(BF16))
    four = dot(two.astype(BF16), two.astype(BF16))
    reach = dot((eye + one).astype(BF16), (eye + two).astype(BF16))
    reach = dot(reach.astype(BF16), (eye + four).astype(BF16))
    return indicator(reach > 0.0)


def kernel(
    n_req, n_tp, chunk,
    lens_s, accepted_s, parents_ref, q_ref, fresh_ref, kv_hbm, residual_hbm, w_hbm,
    hidden_ref, path_ref,
    kv, w, residual, q_in, lens_own, lens_in, out_send, out_in, lse_send, lse_in,
    local_out, local_lse, lse_tile, tree, attention, proj_send, proj_in,
    load_sem, lens_send_sem, lens_recv_sem, q_send_sem, q_recv_sem, o_send_sem, o_recv_sem,
    l_send_sem, l_recv_sem, p_send_sem, p_recv_sem,
):
    me, tp = lax.axis_index("req"), lax.axis_index("tp")
    tokens, width = q_ref.shape
    requests = tokens // TREE
    heads = width // HD
    kv_heads = fresh_ref.shape[1] // (2 * HD)
    pages, page = kv.shape[0], kv.shape[2]
    part = tokens // n_tp
    per_part = part // chunk
    chunks = tokens // chunk
    features = w.shape[1]
    group = heads // kv_heads

    loads = [
        pltpu.make_async_copy(kv_hbm.at[:, p], kv.at[p], load_sem.at[p]) for p in range(pages)
    ]
    loads.append(pltpu.make_async_copy(w_hbm, w, load_sem.at[pages]))
    loads.append(pltpu.make_async_copy(residual_hbm, residual, load_sem.at[pages + 1]))
    for load in loads:
        load.start()

    def ahead(p):
        return lax.rem(me + p, n_req)

    def behind(p):
        return lax.rem(me + n_req - p, n_req)

    barrier = pltpu.get_barrier_semaphore()
    for p in range(1, pages):
        for other in (ahead(p), behind(p)):
            pl.semaphore_signal(barrier, inc=1, device_id={"req": other}, device_id_type=MESH)
    for j in range(1, n_tp):
        pl.semaphore_signal(
            barrier, inc=1, device_id={"tp": lax.rem(tp + j, n_tp)}, device_id_type=MESH
        )

    lens = jnp.zeros((requests, LANES), jnp.int32)
    for r in range(requests):
        lens = jnp.where(iota((requests, LANES), 0) == r, lens_s[r], lens)
    lens_own[...] = lens
    pl.semaphore_wait(barrier, 2 * (pages - 1) + n_tp - 1)

    def first_row(c):
        block = lax.rem(tp + 1 + c // per_part, n_tp)
        return pl.multiple_of(block * part + lax.rem(c, per_part) * chunk, chunk)

    def send_lens(p):
        return pltpu.make_async_remote_copy(
            lens_own, lens_in.at[p - 1], lens_send_sem.at[p - 1], lens_recv_sem.at[p - 1],
            device_id={"req": ahead(p)}, device_id_type=MESH,
        )

    def send_q(p, c):
        rows = pl.ds(first_row(c), chunk)
        return pltpu.make_async_remote_copy(
            q_ref.at[rows], q_in.at[p - 1, rows], q_send_sem.at[p - 1, c], q_recv_sem.at[p - 1, c],
            device_id={"req": ahead(p)}, device_id_type=MESH,
        )

    def send_out(p, c):
        rows = pl.ds(first_row(c), chunk)
        return pltpu.make_async_remote_copy(
            out_send.at[p - 1, rows], out_in.at[p - 1, rows],
            o_send_sem.at[p - 1, c], o_recv_sem.at[p - 1, c],
            device_id={"req": behind(p)}, device_id_type=MESH,
        )

    def send_lse(p, c):
        return pltpu.make_async_remote_copy(
            lse_send.at[p - 1, c], lse_in.at[p - 1, c],
            l_send_sem.at[p - 1, c], l_recv_sem.at[p - 1, c],
            device_id={"req": behind(p)}, device_id_type=MESH,
        )

    def send_proj(j):
        return pltpu.make_async_remote_copy(
            proj_send.at[j], proj_in.at[j], p_send_sem.at[j], p_recv_sem.at[j],
            device_id={"tp": lax.rem(tp + 1 + j, n_tp)}, device_id_type=MESH,
        )

    for p in range(1, pages):
        send_lens(p).start()

    @pl.loop(0, chunks)
    def _(c):
        for p in range(1, pages):
            send_q(p, c).start()

    marked = tree_masks(parents_ref[...], tokens)
    fold = indicator((iota((tokens, TREE), 0) & (TREE - 1)) == iota((tokens, TREE), 1))
    tree[...] = dot(marked, fold)
    accepted = jnp.zeros((requests, tokens), jnp.int32)
    for r in range(requests):
        accepted = jnp.where(iota((requests, tokens), 0) == r, accepted_s[r] + r * TREE, accepted)
    chosen = indicator(iota((requests, tokens), 1) == accepted, F32)
    on_path = dot(chosen, marked.astype(F32))
    upto = indicator(iota((tokens, tokens), 0) <= iota((tokens, tokens), 1), F32)
    count = dot(on_path, upto)
    slots = (requests * PATH, requests)
    spread = indicator((iota(slots, 0) >> 3) == iota(slots, 1), F32)
    slot = (iota((requests * PATH, tokens), 0) & (PATH - 1)).astype(F32) + 1.0
    selector = (dot(spread, count) == slot) & (dot(spread, on_path) > 0.0)
    path_ref[...] = dot(indicator(selector), fresh_ref[...]).astype(BF16)

    lane = iota((TREE, LANES), 1)

    def stacked_queries(ref, rows, k):
        columns = [slice((k * group + g) * HD, (k * group + g + 1) * HD) for g in range(group)]
        return jnp.concatenate([ref[rows, c] for c in columns], axis=0)

    def lens_mask(row, p):
        wide = jnp.concatenate([row] * (page // LANES), axis=1)
        return iota((1, page), 1) + p * page < wide

    ones = jnp.ones((page, HD), BF16)
    units = [(i, k) for i in range(chunk // TREE) for k in range(kv_heads)]

    def key_columns(k):
        return slice(2 * k * HD, (2 * k + 1) * HD)

    def value_columns(k):
        return slice((2 * k + 1) * HD, (2 * k + 2) * HD)

    def with_ones(value_rows):
        return jnp.concatenate([value_rows, ones[: value_rows.shape[0]]], axis=1)

    def by_token(levels, i):
        lse = jnp.zeros((TREE, LANES), F32)
        for k in range(kv_heads):
            for g in range(group):
                level = levels[i * kv_heads + k][g * TREE : (g + 1) * TREE]
                lse = jnp.where(lane == k * group + g, level, lse)
        return lse

    def token_rows(start, i):
        return pl.ds(pl.multiple_of(start + i * TREE, TREE), TREE)

    def local_chunk(start):
        first = start // TREE
        valid = [lens_mask(lens_own[pl.ds(first + i, 1), :], 0) for i in range(chunk // TREE)]
        allowed = [
            jnp.concatenate([tree[token_rows(start, i), :]] * group, axis=0) > 0.0
            for i in range(chunk // TREE)
        ]
        queries = [stacked_queries(q_ref, token_rows(start, i), k) for i, k in units]
        cached = [
            jnp.where(valid[i], dot_t(query, kv[0, first + i, :, key_columns(k)]) * SCALE2, NEGATIVE)
            for query, (i, k) in zip(queries, units)
        ]
        drafted = [
            jnp.where(
                allowed[i],
                dot_t(query, fresh_ref[token_rows(start, i), key_columns(k)]) * SCALE2,
                NEGATIVE,
            )
            for query, (i, k) in zip(queries, units)
        ]
        largest = [
            jnp.maximum(jnp.max(old, axis=1, keepdims=True), jnp.max(new, axis=1, keepdims=True))
            for old, new in zip(cached, drafted)
        ]
        cached = [jnp.exp2(old - top).astype(BF16) for old, top in zip(cached, largest)]
        drafted = [jnp.exp2(new - top).astype(BF16) for new, top in zip(drafted, largest)]
        sums = [
            dot(old, with_ones(kv[0, first + i, :, value_columns(k)]))
            + dot(new, with_ones(fresh_ref[token_rows(start, i), value_columns(k)]))
            for old, new, (i, k) in zip(cached, drafted, units)
        ]
        levels = []
        for both, top, (i, k) in zip(sums, largest, units):
            total = both[:, HD:]
            out = both[:, :HD] / total
            levels.append(top + jnp.log2(total))
            for g in range(group):
                h = k * group + g
                local_out[token_rows(start, i), h * HD : (h + 1) * HD] = out[g * TREE : (g + 1) * TREE]
        for i in range(chunk // TREE):
            local_lse[token_rows(start, i), :] = by_token(levels, i)

    def remote_chunk(start, c, p):
        first = start // TREE
        valid = [lens_mask(lens_in[p - 1, pl.ds(first + i, 1), :], p) for i in range(chunk // TREE)]
        cached = [
            jnp.where(
                valid[i],
                dot_t(
                    stacked_queries(q_in.at[p - 1], token_rows(start, i), k),
                    kv[p, first + i, :, key_columns(k)],
                )
                * SCALE2,
                NEGATIVE,
            )
            for i, k in units
        ]
        largest = [jnp.max(scores, axis=1, keepdims=True) for scores in cached]
        cached = [
            jnp.exp2(scores - jnp.maximum(top, FLOOR)).astype(BF16)
            for scores, top in zip(cached, largest)
        ]
        sums = [
            dot(weights, with_ones(kv[p, first + i, :, value_columns(k)]))
            for weights, (i, k) in zip(cached, units)
        ]
        levels = []
        for both, top, (i, k) in zip(sums, largest, units):
            total = jnp.maximum(both[:, HD:], 1.0)
            out = (both[:, :HD] / total).astype(BF16)
            levels.append(top + jnp.log2(total))
            for g in range(group):
                h = k * group + g
                out_send[p - 1, token_rows(start, i), h * HD : (h + 1) * HD] = out[
                    g * TREE : (g + 1) * TREE
                ]
        for i in range(chunk // TREE):
            lse_tile[i * TREE : (i + 1) * TREE, :] = by_token(levels, i)
        lse_send[p - 1, c] = lse_tile[...].T[:8]

    loads[0].wait()
    local_chunk(first_row(0))
    for p in range(1, pages):
        loads[p].wait()
        send_lens(p).wait_recv()

    @pl.loop(0, chunks)
    def _(c):
        start = first_row(c)
        for p in range(1, pages):
            send_q(p, c).wait_recv()
            remote_chunk(start, c, p)
            send_lse(p, c).start()
            send_out(p, c).start()

        @pl.when(c < chunks - 1)
        def _():
            local_chunk(first_row(c + 1))

    loads[pages].wait()
    loads[pages + 1].wait()

    for j in range(n_tp):

        @pl.loop(0, per_part)
        def _(i):
            c = j * per_part + i
            rows = pl.ds(first_row(c), chunk)
            here = pl.ds(pl.multiple_of(i * chunk, chunk), chunk)
            levels = [local_lse[rows, :]]
            for p in range(1, pages):
                send_lse(p, c).wait_recv()
                send_out(p, c).wait_recv()
                tile = jnp.concatenate(
                    [lse_in[p - 1, c], jnp.zeros((LANES - 8, LANES), F32)], axis=0
                )
                levels.append(tile.T[:chunk])
            largest = functools.reduce(jnp.maximum, levels)
            factors = [jnp.exp2(level - largest) for level in levels]
            inverse = 1.0 / functools.reduce(jnp.add, factors)
            factors = [factor * inverse for factor in factors]
            for h in range(heads):
                columns = slice(h * HD, (h + 1) * HD)
                total = factors[0][:, h : h + 1] * local_out[rows, columns]
                for p in range(1, pages):
                    term = out_in[p - 1, rows, columns].astype(F32)
                    total = total + factors[p][:, h : h + 1] * term
                attention[here, columns] = total.astype(BF16)

        if j == n_tp - 1:
            for other in range(n_tp - 1):
                send_proj(other).wait_recv()
        tile_width = min(features, 1024)

        @pl.loop(0, features // tile_width)
        def _(t):
            columns = pl.ds(pl.multiple_of(t * tile_width, tile_width), tile_width)
            projected = dot(attention[...], w[:, columns]).astype(BF16)
            if j < n_tp - 1:
                proj_send[j, :, columns] = projected
            else:
                summed = projected.astype(F32)
                for other in range(n_tp - 1):
                    summed = summed + proj_in[other, :, columns].astype(F32)
                hidden_ref[:, columns] = (residual[:, columns].astype(F32) + summed).astype(BF16)

        if j < n_tp - 1:
            send_proj(j).start()

    for p in range(1, pages):
        send_lens(p).wait_send()

    @pl.loop(0, chunks)
    def _(c):
        for p in range(1, pages):
            send_q(p, c).wait_send()
            send_lse(p, c).wait_send()
            send_out(p, c).wait_send()

    for j in range(n_tp - 1):
        send_proj(j).wait_send()


def norm_kernel(hidden_ref, gain_ref, path_ref, hidden_out, normed_out, path_out):
    hidden = hidden_ref[...]
    hidden_out[...] = hidden
    wide = hidden.astype(F32)
    mean = jnp.sum(wide * wide, axis=1, keepdims=True) * (1.0 / wide.shape[1])
    normed_out[...] = (wide * lax.rsqrt(mean + 1e-05) * gain_ref[...]).astype(BF16)
    path_out[...] = path_ref[...]


def per_device(n_req, n_tp, queries, new_kv, kv_pool, cache_lens, parents, accepted, residual, w_out, norm_gain):
    requests, pages, page, row_width = kv_pool.shape
    tokens, width = queries.shape
    features = w_out.shape[1]
    part = tokens // n_tp
    chunk = min(part, 2 * TREE)
    chunks = tokens // chunk
    away = pages - 1
    vmem = pl.BlockSpec(memory_space=pltpu.VMEM)
    smem = pl.BlockSpec(memory_space=pltpu.SMEM)
    hbm = pl.BlockSpec(memory_space=pl.ANY)
    dma = pltpu.SemaphoreType.DMA
    hidden, path = pl.pallas_call(
        functools.partial(kernel, n_req, n_tp, chunk),
        out_shape=(
            jax.ShapeDtypeStruct((part, features), BF16),
            jax.ShapeDtypeStruct((requests * PATH, row_width), BF16),
        ),
        in_specs=[smem, smem, vmem, vmem, vmem, hbm, hbm, hbm],
        out_specs=(vmem, vmem),
        scratch_shapes=[
            pltpu.VMEM((pages, requests, page, row_width), BF16),
            pltpu.VMEM(w_out.shape, BF16),
            pltpu.VMEM((part, features), BF16),
            pltpu.VMEM((away, tokens, width), BF16),
            pltpu.VMEM((requests, LANES), jnp.int32),
            pltpu.VMEM((away, requests, LANES), jnp.int32),
            pltpu.VMEM((away, tokens, width), BF16),
            pltpu.VMEM((away, tokens, width), BF16),
            pltpu.VMEM((away, chunks, 8, LANES), F32),
            pltpu.VMEM((away, chunks, 8, LANES), F32),
            pltpu.VMEM((tokens, width), F32),
            pltpu.VMEM((tokens, LANES), F32),
            pltpu.VMEM((LANES, LANES), F32),
            pltpu.VMEM((tokens, TREE), F32),
            pltpu.VMEM((part, width), BF16),
            pltpu.VMEM((max(n_tp - 1, 1), part, features), BF16),
            pltpu.VMEM((max(n_tp - 1, 1), part, features), BF16),
            dma((pages + 2,)),
            dma((away,)),
            dma((away,)),
            dma((away, chunks)),
            dma((away, chunks)),
            dma((away, chunks)),
            dma((away, chunks)),
            dma((away, chunks)),
            dma((away, chunks)),
            dma((max(n_tp - 1, 1),)),
            dma((max(n_tp - 1, 1),)),
        ],
        compiler_params=pltpu.CompilerParams(
            collective_id=0, has_side_effects=True, vmem_limit_bytes=56 * 2**20
        ),
    )(cache_lens, accepted, parents, queries, new_kv, kv_pool, residual, w_out)
    rows = min(part, TREE)
    row_block = pl.BlockSpec((rows, features), lambda i: (i, 0))
    whole_path = pl.BlockSpec(path.shape, lambda i: (0, 0))
    hidden_out, normed, path = pl.pallas_call(
        norm_kernel,
        grid=(part // rows,),
        out_shape=(
            jax.ShapeDtypeStruct(hidden.shape, BF16),
            jax.ShapeDtypeStruct(hidden.shape, BF16),
            jax.ShapeDtypeStruct(path.shape, BF16),
        ),
        in_specs=[row_block, pl.BlockSpec((1, features), lambda i: (0, 0)), whole_path],
        out_specs=(row_block, row_block, whole_path),
    )(hidden, norm_gain.reshape(1, features), path)
    return hidden_out, normed, path.reshape(requests, PATH, row_width)


def solution(mesh):
    placed = (
        P("req", "tp"),
        P("req", "tp"),
        P("req", None, None, "tp"),
        P("req"),
        P("req", None),
        P("req"),
        P(("req", "tp"), None),
        P("tp", None),
        P(),
    )
    return jax.shard_map(
        functools.partial(per_device, mesh.shape["req"], mesh.shape["tp"]),
        mesh=mesh,
        in_specs=placed,
        out_specs=(P(("req", "tp"), None), P(("req", "tp"), None), P("req", None, "tp")),
        check_vma=False,
    )
```

```python
import functools

import jax
import jax.numpy as jnp
from jax import lax
from jax.experimental import pallas as pl
from jax.experimental.pallas import tpu as pltpu
from jax.sharding import PartitionSpec as P

HD = 128
TREE = 32
PATH = 8
LANES = 128
NEGATIVE = -1e30
FLOOR = -1e29
SCALE2 = HD**-0.5 * 1.4426950408889634
MESH = pl.DeviceIdType.MESH
F32 = jnp.float32
BF16 = jnp.bfloat16


def iota(shape, axis):
    return lax.broadcasted_iota(jnp.int32, shape, axis)


def dot(left, right):
    return jnp.dot(left, right, preferred_element_type=F32)


def dot_t(left, right):
    return lax.dot_general(left, right, (((1,), (1,)), ((), ())), preferred_element_type=F32)


def indicator(mask, dtype=BF16):
    return jnp.where(mask, 1.0, 0.0).astype(dtype)


def tree_masks(parents, tokens):
    requests = tokens // TREE
    expand = indicator((iota((tokens, requests), 0) >> 5) == iota((tokens, requests), 1), F32)
    spread = dot(expand, parents.astype(F32))
    pick = (iota((tokens, TREE), 0) & (TREE - 1)) == iota((tokens, TREE), 1)
    parent = jnp.sum(jnp.where(pick, spread, 0.0), axis=1, keepdims=True)
    rows, columns = iota((tokens, tokens), 0), iota((tokens, tokens), 1)
    base = (rows & ~(TREE - 1)).astype(F32)
    one = indicator(columns.astype(F32) == parent + base, F32)
    eye = indicator(rows == columns, F32)
    two = dot(one.astype(BF16), one.astype(BF16))
    four = dot(two.astype(BF16), two.astype(BF16))
    reach = dot((eye + one).astype(BF16), (eye + two).astype(BF16))
    reach = dot(reach.astype(BF16), (eye + four).astype(BF16))
    return indicator(reach > 0.0)


def kernel(
    n_req, n_tp, chunk,
    lens_s, accepted_s, parents_ref, q_ref, fresh_ref, kv_hbm, residual_hbm, w_hbm,
    hidden_ref, path_ref,
    kv, w, residual, q_in, lens_own, lens_in, out_send, out_in, lse_send, lse_in,
    local_out, local_lse, lse_tile, tree, attention, proj_send, proj_in,
    q_relay, lens_relay, out_relay, out_far, lse_relay, lse_far,
    load_sem, lens_send_sem, lens_recv_sem, q_send_sem, q_recv_sem, o_send_sem, o_recv_sem,
    l_send_sem, l_recv_sem, p_send_sem, p_recv_sem,
    zn_send_sem, zn_recv_sem, zq_send_sem, zq_recv_sem, zo_send_sem, zo_recv_sem,
    zl_send_sem, zl_recv_sem,
):
    me, tp = lax.axis_index("req"), lax.axis_index("tp")
    tokens, width = q_ref.shape
    requests = tokens // TREE
    heads = width // HD
    kv_heads = fresh_ref.shape[1] // (2 * HD)
    pages, page = kv.shape[0], kv.shape[2]
    part = tokens // n_tp
    per_part = part // chunk
    chunks = tokens // chunk
    features = w.shape[1]
    group = heads // kv_heads

    loads = [
        pltpu.make_async_copy(kv_hbm.at[:, p], kv.at[p], load_sem.at[p]) for p in range(pages)
    ]
    loads.append(pltpu.make_async_copy(w_hbm, w, load_sem.at[pages]))
    loads.append(pltpu.make_async_copy(residual_hbm, residual, load_sem.at[pages + 1]))
    for load in loads:
        load.start()

    place = lax.rem(me, pages)
    layer = me - place
    above = lax.rem(me + pages, n_req)
    below = lax.rem(me + n_req - pages, n_req)

    def ahead(p):
        return layer + lax.rem(place + p, pages)

    def behind(p):
        return layer + lax.rem(place + pages - p, pages)

    def if_near(p, action):
        pl.when(place + p < pages)(action)

    def if_far(p, action):
        pl.when(place + p >= pages)(action)

    barrier = pltpu.get_barrier_semaphore()
    for other in [ahead(p) for p in range(1, pages)] + [above, below]:
        pl.semaphore_signal(barrier, inc=1, device_id={"req": other}, device_id_type=MESH)
    for j in range(1, n_tp):
        pl.semaphore_signal(
            barrier, inc=1, device_id={"tp": lax.rem(tp + j, n_tp)}, device_id_type=MESH
        )

    lens = jnp.zeros((requests, LANES), jnp.int32)
    for r in range(requests):
        lens = jnp.where(iota((requests, LANES), 0) == r, lens_s[r], lens)
    lens_own[...] = lens
    pl.semaphore_wait(barrier, pages + 1 + n_tp - 1)

    def first_row(c):
        block = lax.rem(tp + 1 + c // per_part, n_tp)
        return pl.multiple_of(block * part + lax.rem(c, per_part) * chunk, chunk)

    def send_lens(p, source=lens_own):
        return pltpu.make_async_remote_copy(
            source, lens_in.at[p - 1], lens_send_sem.at[p - 1], lens_recv_sem.at[p - 1],
            device_id={"req": ahead(p)}, device_id_type=MESH,
        )

    def send_q(p, c, source=q_ref):
        rows = pl.ds(first_row(c), chunk)
        return pltpu.make_async_remote_copy(
            source.at[rows], q_in.at[p - 1, rows], q_send_sem.at[p - 1, c], q_recv_sem.at[p - 1, c],
            device_id={"req": ahead(p)}, device_id_type=MESH,
        )

    def send_out(p, c):
        rows = pl.ds(first_row(c), chunk)
        return pltpu.make_async_remote_copy(
            out_send.at[p - 1, rows], out_in.at[p - 1, rows],
            o_send_sem.at[p - 1, c], o_recv_sem.at[p - 1, c],
            device_id={"req": behind(p)}, device_id_type=MESH,
        )

    def send_lse(p, c):
        return pltpu.make_async_remote_copy(
            lse_send.at[p - 1, c], lse_in.at[p - 1, c],
            l_send_sem.at[p - 1, c], l_recv_sem.at[p - 1, c],
            device_id={"req": behind(p)}, device_id_type=MESH,
        )

    def send_proj(j):
        return pltpu.make_async_remote_copy(
            proj_send.at[j], proj_in.at[j], p_send_sem.at[j], p_recv_sem.at[j],
            device_id={"tp": lax.rem(tp + 1 + j, n_tp)}, device_id_type=MESH,
        )

    def cross_lens():
        return pltpu.make_async_remote_copy(
            lens_own, lens_relay, zn_send_sem, zn_recv_sem,
            device_id={"req": above}, device_id_type=MESH,
        )

    def cross_q(c):
        rows = pl.ds(first_row(c), chunk)
        return pltpu.make_async_remote_copy(
            q_ref.at[rows], q_relay.at[rows], zq_send_sem.at[c], zq_recv_sem.at[c],
            device_id={"req": above}, device_id_type=MESH,
        )

    def cross_out(c):
        rows = pl.ds(first_row(c), chunk)
        return pltpu.make_async_remote_copy(
            out_relay.at[rows], out_far.at[rows], zo_send_sem.at[c], zo_recv_sem.at[c],
            device_id={"req": below}, device_id_type=MESH,
        )

    def cross_lse(c):
        return pltpu.make_async_remote_copy(
            lse_relay.at[c], lse_far.at[c], zl_send_sem.at[c], zl_recv_sem.at[c],
            device_id={"req": below}, device_id_type=MESH,
        )

    cross_lens().start()
    for p in range(1, pages):
        if_near(p, lambda p=p: send_lens(p).start())

    @pl.loop(0, chunks)
    def _(c):
        cross_q(c).start()
        for p in range(1, pages):
            if_near(p, lambda p=p: send_q(p, c).start())

    def pass_on(c):
        cross_q(c).wait_recv()
        for p in range(1, pages):
            if_far(p, lambda p=p: send_q(p, c, q_relay).start())

    marked = tree_masks(parents_ref[...], tokens)
    fold = indicator((iota((tokens, TREE), 0) & (TREE - 1)) == iota((tokens, TREE), 1))
    tree[...] = dot(marked, fold)
    accepted = jnp.zeros((requests, tokens), jnp.int32)
    for r in range(requests):
        accepted = jnp.where(iota((requests, tokens), 0) == r, accepted_s[r] + r * TREE, accepted)
    chosen = indicator(iota((requests, tokens), 1) == accepted, F32)
    on_path = dot(chosen, marked.astype(F32))
    upto = indicator(iota((tokens, tokens), 0) <= iota((tokens, tokens), 1), F32)
    count = dot(on_path, upto)
    slots = (requests * PATH, requests)
    spread = indicator((iota(slots, 0) >> 3) == iota(slots, 1), F32)
    slot = (iota((requests * PATH, tokens), 0) & (PATH - 1)).astype(F32) + 1.0
    selector = (dot(spread, count) == slot) & (dot(spread, on_path) > 0.0)
    path_ref[...] = dot(indicator(selector), fresh_ref[...]).astype(BF16)

    lane = iota((TREE, LANES), 1)

    def stacked_queries(ref, rows, k):
        columns = [slice((k * group + g) * HD, (k * group + g + 1) * HD) for g in range(group)]
        return jnp.concatenate([ref[rows, c] for c in columns], axis=0)

    def lens_mask(row, p):
        wide = jnp.concatenate([row] * (page // LANES), axis=1)
        return iota((1, page), 1) + p * page < wide

    ones = jnp.ones((page, HD), BF16)
    units = [(i, k) for i in range(chunk // TREE) for k in range(kv_heads)]

    def key_columns(k):
        return slice(2 * k * HD, (2 * k + 1) * HD)

    def value_columns(k):
        return slice((2 * k + 1) * HD, (2 * k + 2) * HD)

    def with_ones(value_rows):
        return jnp.concatenate([value_rows, ones[: value_rows.shape[0]]], axis=1)

    def by_token(levels, i):
        lse = jnp.zeros((TREE, LANES), F32)
        for k in range(kv_heads):
            for g in range(group):
                level = levels[i * kv_heads + k][g * TREE : (g + 1) * TREE]
                lse = jnp.where(lane == k * group + g, level, lse)
        return lse

    def token_rows(start, i):
        return pl.ds(pl.multiple_of(start + i * TREE, TREE), TREE)

    def local_chunk(start):
        first = start // TREE
        valid = [lens_mask(lens_own[pl.ds(first + i, 1), :], 0) for i in range(chunk // TREE)]
        allowed = [
            jnp.concatenate([tree[token_rows(start, i), :]] * group, axis=0) > 0.0
            for i in range(chunk // TREE)
        ]
        queries = [stacked_queries(q_ref, token_rows(start, i), k) for i, k in units]
        cached = [
            jnp.where(valid[i], dot_t(query, kv[0, first + i, :, key_columns(k)]) * SCALE2, NEGATIVE)
            for query, (i, k) in zip(queries, units)
        ]
        drafted = [
            jnp.where(
                allowed[i],
                dot_t(query, fresh_ref[token_rows(start, i), key_columns(k)]) * SCALE2,
                NEGATIVE,
            )
            for query, (i, k) in zip(queries, units)
        ]
        largest = [
            jnp.maximum(jnp.max(old, axis=1, keepdims=True), jnp.max(new, axis=1, keepdims=True))
            for old, new in zip(cached, drafted)
        ]
        cached = [jnp.exp2(old - top).astype(BF16) for old, top in zip(cached, largest)]
        drafted = [jnp.exp2(new - top).astype(BF16) for new, top in zip(drafted, largest)]
        sums = [
            dot(old, with_ones(kv[0, first + i, :, value_columns(k)]))
            + dot(new, with_ones(fresh_ref[token_rows(start, i), value_columns(k)]))
            for old, new, (i, k) in zip(cached, drafted, units)
        ]
        levels = []
        for both, top, (i, k) in zip(sums, largest, units):
            total = both[:, HD:]
            out = both[:, :HD] / total
            levels.append(top + jnp.log2(total))
            for g in range(group):
                h = k * group + g
                local_out[token_rows(start, i), h * HD : (h + 1) * HD] = out[g * TREE : (g + 1) * TREE]
        for i in range(chunk // TREE):
            local_lse[token_rows(start, i), :] = by_token(levels, i)

    def remote_chunk(start, c, p):
        first = start // TREE
        valid = [lens_mask(lens_in[p - 1, pl.ds(first + i, 1), :], p) for i in range(chunk // TREE)]
        cached = [
            jnp.where(
                valid[i],
                dot_t(
                    stacked_queries(q_in.at[p - 1], token_rows(start, i), k),
                    kv[p, first + i, :, key_columns(k)],
                )
                * SCALE2,
                NEGATIVE,
            )
            for i, k in units
        ]
        largest = [jnp.max(scores, axis=1, keepdims=True) for scores in cached]
        cached = [
            jnp.exp2(scores - jnp.maximum(top, FLOOR)).astype(BF16)
            for scores, top in zip(cached, largest)
        ]
        sums = [
            dot(weights, with_ones(kv[p, first + i, :, value_columns(k)]))
            for weights, (i, k) in zip(cached, units)
        ]
        levels = []
        for both, top, (i, k) in zip(sums, largest, units):
            total = jnp.maximum(both[:, HD:], 1.0)
            out = (both[:, :HD] / total).astype(BF16)
            levels.append(top + jnp.log2(total))
            for g in range(group):
                h = k * group + g
                out_send[p - 1, token_rows(start, i), h * HD : (h + 1) * HD] = out[
                    g * TREE : (g + 1) * TREE
                ]
        for i in range(chunk // TREE):
            lse_tile[i * TREE : (i + 1) * TREE, :] = by_token(levels, i)
        lse_send[p - 1, c] = lse_tile[...].T[:8]

    def by_row(compact):
        tile = jnp.concatenate([compact, jnp.zeros((LANES - 8, LANES), F32)], axis=0)
        return tile.T[:chunk]

    def near_levels(c, near):
        levels = []
        for p in range(1, pages):
            wanted = (place + p < pages) if near else (place + p >= pages)
            levels.append(jnp.where(wanted, lse_in[p - 1, c], NEGATIVE))
        return levels

    def merge_far(c):
        rows = pl.ds(first_row(c), chunk)
        for p in range(1, pages):
            send_lse(p, c).wait_recv()
            send_out(p, c).wait_recv()
        levels = near_levels(c, False)
        largest = functools.reduce(jnp.maximum, levels)
        factors = [jnp.exp2(level - largest) for level in levels]
        total = functools.reduce(jnp.add, factors)
        lse_relay[c] = largest + jnp.log2(total)
        factors = [by_row(factor / total) for factor in factors]
        for h in range(heads):
            columns = slice(h * HD, (h + 1) * HD)
            terms = [
                factors[p - 1][:, h : h + 1] * out_in[p - 1, rows, columns].astype(F32)
                for p in range(1, pages)
            ]
            out_relay[rows, columns] = functools.reduce(jnp.add, terms).astype(BF16)
        cross_lse(c).start()
        cross_out(c).start()

    cross_lens().wait_recv()
    for p in range(1, pages):
        if_far(p, lambda p=p: send_lens(p, lens_relay).start())
    pass_on(0)
    loads[0].wait()
    local_chunk(first_row(0))
    for p in range(1, pages):
        loads[p].wait()
        send_lens(p).wait_recv()

    @pl.loop(0, chunks)
    def _(c):
        start = first_row(c)

        @pl.when(c < chunks - 1)
        def _():
            pass_on(c + 1)

        for p in range(1, pages):
            send_q(p, c).wait_recv()
            remote_chunk(start, c, p)
            send_lse(p, c).start()
            send_out(p, c).start()

        @pl.when(c < chunks - 1)
        def _():
            local_chunk(first_row(c + 1))

        @pl.when(c > 0)
        def _():
            merge_far(c - 1)

    merge_far(chunks - 1)

    loads[pages].wait()
    loads[pages + 1].wait()

    for j in range(n_tp):

        @pl.loop(0, per_part)
        def _(i):
            c = j * per_part + i
            rows = pl.ds(first_row(c), chunk)
            here = pl.ds(pl.multiple_of(i * chunk, chunk), chunk)
            cross_lse(c).wait_recv()
            cross_out(c).wait_recv()
            levels = [local_lse[rows, :], by_row(lse_far[c])]
            levels += [by_row(level) for level in near_levels(c, True)]
            largest = functools.reduce(jnp.maximum, levels)
            factors = [jnp.exp2(level - largest) for level in levels]
            inverse = 1.0 / functools.reduce(jnp.add, factors)
            factors = [factor * inverse for factor in factors]
            for h in range(heads):
                columns = slice(h * HD, (h + 1) * HD)
                total = factors[0][:, h : h + 1] * local_out[rows, columns]
                terms = [out_far[rows, columns]]
                terms += [out_in[p - 1, rows, columns] for p in range(1, pages)]
                for factor, term in zip(factors[1:], terms):
                    total = total + factor[:, h : h + 1] * term.astype(F32)
                attention[here, columns] = total.astype(BF16)

        if j == n_tp - 1:
            for other in range(n_tp - 1):
                send_proj(other).wait_recv()
        tile_width = min(features, 1024)

        @pl.loop(0, features // tile_width)
        def _(t):
            columns = pl.ds(pl.multiple_of(t * tile_width, tile_width), tile_width)
            projected = dot(attention[...], w[:, columns]).astype(BF16)
            if j < n_tp - 1:
                proj_send[j, :, columns] = projected
            else:
                summed = projected.astype(F32)
                for other in range(n_tp - 1):
                    summed = summed + proj_in[other, :, columns].astype(F32)
                hidden_ref[:, columns] = (residual[:, columns].astype(F32) + summed).astype(BF16)

        if j < n_tp - 1:
            send_proj(j).start()

    for p in range(1, pages):
        send_lens(p).wait_send()

    cross_lens().wait_send()

    @pl.loop(0, chunks)
    def _(c):
        cross_q(c).wait_send()
        cross_lse(c).wait_send()
        cross_out(c).wait_send()
        for p in range(1, pages):
            send_q(p, c).wait_send()
            send_lse(p, c).wait_send()
            send_out(p, c).wait_send()

    for j in range(n_tp - 1):
        send_proj(j).wait_send()


def norm_kernel(hidden_ref, gain_ref, path_ref, hidden_out, normed_out, path_out):
    hidden = hidden_ref[...]
    hidden_out[...] = hidden
    wide = hidden.astype(F32)
    mean = jnp.sum(wide * wide, axis=1, keepdims=True) * (1.0 / wide.shape[1])
    normed_out[...] = (wide * lax.rsqrt(mean + 1e-05) * gain_ref[...]).astype(BF16)
    path_out[...] = path_ref[...]


def per_device(n_req, n_tp, queries, new_kv, kv_pool, cache_lens, parents, accepted, residual, w_out, norm_gain):
    requests, pages, page, row_width = kv_pool.shape
    tokens, width = queries.shape
    features = w_out.shape[1]
    part = tokens // n_tp
    chunk = min(part, 2 * TREE)
    chunks = tokens // chunk
    away = pages - 1
    vmem = pl.BlockSpec(memory_space=pltpu.VMEM)
    smem = pl.BlockSpec(memory_space=pltpu.SMEM)
    hbm = pl.BlockSpec(memory_space=pl.ANY)
    dma = pltpu.SemaphoreType.DMA
    hidden, path = pl.pallas_call(
        functools.partial(kernel, n_req, n_tp, chunk),
        out_shape=(
            jax.ShapeDtypeStruct((part, features), BF16),
            jax.ShapeDtypeStruct((requests * PATH, row_width), BF16),
        ),
        in_specs=[smem, smem, vmem, vmem, vmem, hbm, hbm, hbm],
        out_specs=(vmem, vmem),
        scratch_shapes=[
            pltpu.VMEM((pages, requests, page, row_width), BF16),
            pltpu.VMEM(w_out.shape, BF16),
            pltpu.VMEM((part, features), BF16),
            pltpu.VMEM((away, tokens, width), BF16),
            pltpu.VMEM((requests, LANES), jnp.int32),
            pltpu.VMEM((away, requests, LANES), jnp.int32),
            pltpu.VMEM((away, tokens, width), BF16),
            pltpu.VMEM((away, tokens, width), BF16),
            pltpu.VMEM((away, chunks, 8, LANES), F32),
            pltpu.VMEM((away, chunks, 8, LANES), F32),
            pltpu.VMEM((tokens, width), F32),
            pltpu.VMEM((tokens, LANES), F32),
            pltpu.VMEM((LANES, LANES), F32),
            pltpu.VMEM((tokens, TREE), F32),
            pltpu.VMEM((part, width), BF16),
            pltpu.VMEM((max(n_tp - 1, 1), part, features), BF16),
            pltpu.VMEM((max(n_tp - 1, 1), part, features), BF16),
            pltpu.VMEM((tokens, width), BF16),
            pltpu.VMEM((requests, LANES), jnp.int32),
            pltpu.VMEM((tokens, width), BF16),
            pltpu.VMEM((tokens, width), BF16),
            pltpu.VMEM((chunks, 8, LANES), F32),
            pltpu.VMEM((chunks, 8, LANES), F32),
            dma((pages + 2,)),
            dma((away,)),
            dma((away,)),
            dma((away, chunks)),
            dma((away, chunks)),
            dma((away, chunks)),
            dma((away, chunks)),
            dma((away, chunks)),
            dma((away, chunks)),
            dma((max(n_tp - 1, 1),)),
            dma((max(n_tp - 1, 1),)),
            dma,
            dma,
            dma((chunks,)),
            dma((chunks,)),
            dma((chunks,)),
            dma((chunks,)),
            dma((chunks,)),
            dma((chunks,)),
        ],
        compiler_params=pltpu.CompilerParams(
            collective_id=0, has_side_effects=True, vmem_limit_bytes=56 * 2**20
        ),
    )(cache_lens, accepted, parents, queries, new_kv, kv_pool, residual, w_out)
    rows = min(part, TREE)
    row_block = pl.BlockSpec((rows, features), lambda i: (i, 0))
    whole_path = pl.BlockSpec(path.shape, lambda i: (0, 0))
    hidden_out, normed, path = pl.pallas_call(
        norm_kernel,
        grid=(part // rows,),
        out_shape=(
            jax.ShapeDtypeStruct(hidden.shape, BF16),
            jax.ShapeDtypeStruct(hidden.shape, BF16),
            jax.ShapeDtypeStruct(path.shape, BF16),
        ),
        in_specs=[row_block, pl.BlockSpec((1, features), lambda i: (0, 0)), whole_path],
        out_specs=(row_block, row_block, whole_path),
    )(hidden, norm_gain.reshape(1, features), path)
    return hidden_out, normed, path.reshape(requests, PATH, row_width)


def solution(mesh):
    placed = (
        P("req", "tp"),
        P("req", "tp"),
        P("req", None, None, "tp"),
        P("req"),
        P("req", None),
        P("req"),
        P(("req", "tp"), None),
        P("tp", None),
        P(),
    )
    return jax.shard_map(
        functools.partial(per_device, mesh.shape["req"], mesh.shape["tp"]),
        mesh=mesh,
        in_specs=placed,
        out_specs=(P(("req", "tp"), None), P(("req", "tp"), None), P("req", None, "tp")),
        check_vma=False,
    )
```

```python
import functools

import jax
import jax.numpy as jnp
from jax import lax
from jax.experimental import pallas as pl
from jax.experimental.pallas import tpu as pltpu
from jax.sharding import PartitionSpec as P

HD = 128
TREE = 32
PATH = 8
LANES = 128
NEGATIVE = -1e30
FLOOR = -1e29
SCALE2 = HD**-0.5 * 1.4426950408889634
MESH = pl.DeviceIdType.MESH
F32 = jnp.float32
BF16 = jnp.bfloat16


def iota(shape, axis):
    return lax.broadcasted_iota(jnp.int32, shape, axis)


def dot(left, right):
    return jnp.dot(left, right, preferred_element_type=F32)


def dot_t(left, right):
    return lax.dot_general(left, right, (((1,), (1,)), ((), ())), preferred_element_type=F32)


def indicator(mask, dtype=BF16):
    return jnp.where(mask, 1.0, 0.0).astype(dtype)


def tree_masks(parents, tokens):
    requests = tokens // TREE
    expand = indicator((iota((tokens, requests), 0) >> 5) == iota((tokens, requests), 1), F32)
    spread = dot(expand, parents.astype(F32))
    pick = (iota((tokens, TREE), 0) & (TREE - 1)) == iota((tokens, TREE), 1)
    parent = jnp.sum(jnp.where(pick, spread, 0.0), axis=1, keepdims=True)
    rows, columns = iota((tokens, tokens), 0), iota((tokens, tokens), 1)
    base = (rows & ~(TREE - 1)).astype(F32)
    one = indicator(columns.astype(F32) == parent + base, F32)
    eye = indicator(rows == columns, F32)
    two = dot(one.astype(BF16), one.astype(BF16))
    four = dot(two.astype(BF16), two.astype(BF16))
    reach = dot((eye + one).astype(BF16), (eye + two).astype(BF16))
    reach = dot(reach.astype(BF16), (eye + four).astype(BF16))
    return indicator(reach > 0.0)


def kernel(
    n_req, n_tp, chunk,
    lens_s, accepted_s, parents_ref, q_hbm, fresh_hbm, kv_hbm, residual_hbm, w_hbm,
    hidden_ref, path_ref,
    q_ref, fresh_ref, kv, w, residual, q_in, lens_own, lens_in, out_send, out_in, lse_send, lse_in,
    local_out, local_lse, tree, attention, proj_send, proj_in,
    load_sem, lens_send_sem, lens_recv_sem, q_send_sem, q_recv_sem, o_send_sem, o_recv_sem,
    l_send_sem, l_recv_sem, p_send_sem, p_recv_sem,
):
    me, tp = lax.axis_index("req"), lax.axis_index("tp")
    tokens, width = q_ref.shape
    requests = tokens // TREE
    heads = width // HD
    kv_heads = fresh_ref.shape[1] // (2 * HD)
    pages, page = kv.shape[0], kv.shape[2]
    part = tokens // n_tp
    per_part = part // chunk
    chunks = tokens // chunk
    features = w.shape[1]
    group = heads // kv_heads

    first_loads = [
        pltpu.make_async_copy(fresh_hbm, fresh_ref, load_sem.at[pages + 2]),
        pltpu.make_async_copy(q_hbm, q_ref, load_sem.at[pages + 3]),
    ]
    loads = [
        pltpu.make_async_copy(kv_hbm.at[:, p], kv.at[p], load_sem.at[p]) for p in range(pages)
    ]
    loads.append(pltpu.make_async_copy(w_hbm, w, load_sem.at[pages]))
    loads.append(pltpu.make_async_copy(residual_hbm, residual, load_sem.at[pages + 1]))
    for load in first_loads + loads:
        load.start()

    def ahead(p):
        return lax.rem(me + p, n_req)

    def behind(p):
        return lax.rem(me + n_req - p, n_req)

    barrier = pltpu.get_barrier_semaphore()
    for p in range(1, pages):
        for other in (ahead(p), behind(p)):
            pl.semaphore_signal(barrier, inc=1, device_id={"req": other}, device_id_type=MESH)
    for j in range(1, n_tp):
        pl.semaphore_signal(
            barrier, inc=1, device_id={"tp": lax.rem(tp + j, n_tp)}, device_id_type=MESH
        )

    lens = jnp.zeros((requests, LANES), jnp.int32)
    for r in range(requests):
        lens = jnp.where(iota((requests, LANES), 0) == r, lens_s[r], lens)
    lens_own[...] = lens
    pl.semaphore_wait(barrier, 2 * (pages - 1) + n_tp - 1)

    def first_row(c):
        block = lax.rem(tp + 1 + c // per_part, n_tp)
        return pl.multiple_of(block * part + lax.rem(c, per_part) * chunk, chunk)

    def send_lens(p):
        return pltpu.make_async_remote_copy(
            lens_own, lens_in.at[p - 1], lens_send_sem.at[p - 1], lens_recv_sem.at[p - 1],
            device_id={"req": ahead(p)}, device_id_type=MESH,
        )

    def send_q(p, c):
        rows = pl.ds(first_row(c), chunk)
        return pltpu.make_async_remote_copy(
            q_hbm.at[rows], q_in.at[p - 1, rows], q_send_sem.at[p - 1, c], q_recv_sem.at[p - 1, c],
            device_id={"req": ahead(p)}, device_id_type=MESH,
        )

    def send_out(p, c):
        rows = pl.ds(first_row(c), chunk)
        return pltpu.make_async_remote_copy(
            out_send.at[p - 1, rows], out_in.at[p - 1, rows],
            o_send_sem.at[p - 1, c], o_recv_sem.at[p - 1, c],
            device_id={"req": behind(p)}, device_id_type=MESH,
        )

    def send_lse(p, c):
        return pltpu.make_async_remote_copy(
            lse_send.at[p - 1, c], lse_in.at[p - 1, c],
            l_send_sem.at[p - 1, c], l_recv_sem.at[p - 1, c],
            device_id={"req": behind(p)}, device_id_type=MESH,
        )

    def send_proj(j):
        return pltpu.make_async_remote_copy(
            proj_send.at[j], proj_in.at[j], p_send_sem.at[j], p_recv_sem.at[j],
            device_id={"tp": lax.rem(tp + 1 + j, n_tp)}, device_id_type=MESH,
        )

    for p in range(1, pages):
        send_lens(p).start()

    upfront = chunks // 2

    @pl.loop(0, upfront)
    def _(c):
        for p in range(1, pages):
            send_q(p, c).start()

    marked = tree_masks(parents_ref[...], tokens)
    fold = indicator((iota((tokens, TREE), 0) & (TREE - 1)) == iota((tokens, TREE), 1))
    tree[...] = dot(marked, fold)
    accepted = jnp.zeros((requests, tokens), jnp.int32)
    for r in range(requests):
        accepted = jnp.where(iota((requests, tokens), 0) == r, accepted_s[r] + r * TREE, accepted)
    chosen = indicator(iota((requests, tokens), 1) == accepted, F32)
    on_path = dot(chosen, marked.astype(F32))
    upto = indicator(iota((tokens, tokens), 0) <= iota((tokens, tokens), 1), F32)
    count = dot(on_path, upto)
    slots = (requests * PATH, requests)
    spread = indicator((iota(slots, 0) >> 3) == iota(slots, 1), F32)
    slot = (iota((requests * PATH, tokens), 0) & (PATH - 1)).astype(F32) + 1.0
    selector = (dot(spread, count) == slot) & (dot(spread, on_path) > 0.0)
    first_loads[0].wait()
    path_ref[...] = dot(indicator(selector), fresh_ref[...]).astype(BF16)

    lane = iota((TREE, LANES), 1)

    def stacked_queries(ref, rows, k):
        columns = [slice((k * group + g) * HD, (k * group + g + 1) * HD) for g in range(group)]
        return jnp.concatenate([ref[rows, c] for c in columns], axis=0)

    def lens_mask(row, p):
        wide = jnp.concatenate([row] * (page // LANES), axis=1)
        return iota((1, page), 1) + p * page < wide

    ones = jnp.ones((page, HD), BF16)
    units = [(i, k) for i in range(chunk // TREE) for k in range(kv_heads)]

    def key_columns(k):
        return slice(2 * k * HD, (2 * k + 1) * HD)

    def value_columns(k):
        return slice((2 * k + 1) * HD, (2 * k + 2) * HD)

    def with_ones(value_rows):
        return jnp.concatenate([value_rows, ones[: value_rows.shape[0]]], axis=1)

    def by_token(levels, i):
        lse = jnp.zeros((TREE, LANES), F32)
        for k in range(kv_heads):
            for g in range(group):
                level = levels[i * kv_heads + k][g * TREE : (g + 1) * TREE]
                lse = jnp.where(lane == k * group + g, level, lse)
        return lse

    def token_rows(start, i):
        return pl.ds(pl.multiple_of(start + i * TREE, TREE), TREE)

    def local_chunk(start):
        first = start // TREE
        valid = [lens_mask(lens_own[pl.ds(first + i, 1), :], 0) for i in range(chunk // TREE)]
        allowed = [
            jnp.concatenate([tree[token_rows(start, i), :]] * group, axis=0) > 0.0
            for i in range(chunk // TREE)
        ]
        queries = [stacked_queries(q_ref, token_rows(start, i), k) for i, k in units]
        cached = [
            jnp.where(valid[i], dot_t(query, kv[0, first + i, :, key_columns(k)]) * SCALE2, NEGATIVE)
            for query, (i, k) in zip(queries, units)
        ]
        drafted = [
            jnp.where(
                allowed[i],
                dot_t(query, fresh_ref[token_rows(start, i), key_columns(k)]) * SCALE2,
                NEGATIVE,
            )
            for query, (i, k) in zip(queries, units)
        ]
        largest = [
            jnp.maximum(jnp.max(old, axis=1, keepdims=True), jnp.max(new, axis=1, keepdims=True))
            for old, new in zip(cached, drafted)
        ]
        cached = [jnp.exp2(old - top).astype(BF16) for old, top in zip(cached, largest)]
        drafted = [jnp.exp2(new - top).astype(BF16) for new, top in zip(drafted, largest)]
        sums = [
            dot(old, with_ones(kv[0, first + i, :, value_columns(k)]))
            + dot(new, with_ones(fresh_ref[token_rows(start, i), value_columns(k)]))
            for old, new, (i, k) in zip(cached, drafted, units)
        ]
        levels = []
        for both, top, (i, k) in zip(sums, largest, units):
            total = both[:, HD:]
            out = both[:, :HD] / total
            levels.append(top + jnp.log2(total))
            for g in range(group):
                h = k * group + g
                local_out[token_rows(start, i), h * HD : (h + 1) * HD] = out[g * TREE : (g + 1) * TREE]
        for i in range(chunk // TREE):
            local_lse[token_rows(start, i), :] = by_token(levels, i)

    away = [(p, i, k) for p in range(1, pages) for i, k in units]

    def remote_chunk(start, c):
        first = start // TREE
        valid = {
            (p, i): lens_mask(lens_in[p - 1, pl.ds(first + i, 1), :], p)
            for p in range(1, pages)
            for i in range(chunk // TREE)
        }
        cached = [
            jnp.where(
                valid[p, i],
                dot_t(
                    stacked_queries(q_in.at[p - 1], token_rows(start, i), k),
                    kv[p, first + i, :, key_columns(k)],
                )
                * SCALE2,
                NEGATIVE,
            )
            for p, i, k in away
        ]
        largest = [jnp.max(scores, axis=1, keepdims=True) for scores in cached]
        cached = [
            jnp.exp2(scores - jnp.maximum(top, FLOOR)).astype(BF16)
            for scores, top in zip(cached, largest)
        ]
        sums = [
            dot(weights, with_ones(kv[p, first + i, :, value_columns(k)]))
            for weights, (p, i, k) in zip(cached, away)
        ]
        levels = []
        for both, top, (p, i, k) in zip(sums, largest, away):
            total = jnp.maximum(both[:, HD:], 1.0)
            out = (both[:, :HD] / total).astype(BF16)
            levels.append(top + jnp.log2(total))
            for g in range(group):
                h = k * group + g
                out_send[p - 1, token_rows(start, i), h * HD : (h + 1) * HD] = out[
                    g * TREE : (g + 1) * TREE
                ]
        for p in range(1, pages):
            some = levels[(p - 1) * len(units) : p * len(units)]
            rows = [by_token(some, i) for i in range(chunk // TREE)]
            rows.append(jnp.zeros((LANES - chunk, LANES), F32))
            lse_send[p - 1, c] = jnp.concatenate(rows, axis=0).T[:8]

    first_loads[1].wait()
    loads[0].wait()
    local_chunk(first_row(0))
    for p in range(1, pages):
        loads[p].wait()
        send_lens(p).wait_recv()

    @pl.loop(0, chunks)
    def _(c):
        @pl.when(c < chunks - upfront)
        def _():
            for p in range(1, pages):
                send_q(p, c + upfront).start()

        for p in range(1, pages):
            send_q(p, c).wait_recv()
        remote_chunk(first_row(c), c)
        for p in range(1, pages):
            send_lse(p, c).start()
            send_out(p, c).start()

        @pl.when(c < chunks - 1)
        def _():
            local_chunk(first_row(c + 1))

    loads[pages].wait()
    loads[pages + 1].wait()

    for j in range(n_tp):

        @pl.loop(0, per_part)
        def _(i):
            c = j * per_part + i
            rows = pl.ds(first_row(c), chunk)
            here = pl.ds(pl.multiple_of(i * chunk, chunk), chunk)
            levels = [local_lse[rows, :]]
            for p in range(1, pages):
                send_lse(p, c).wait_recv()
                send_out(p, c).wait_recv()
                tile = jnp.concatenate(
                    [lse_in[p - 1, c], jnp.zeros((LANES - 8, LANES), F32)], axis=0
                )
                levels.append(tile.T[:chunk])
            largest = functools.reduce(jnp.maximum, levels)
            factors = [jnp.exp2(level - largest) for level in levels]
            inverse = 1.0 / functools.reduce(jnp.add, factors)
            factors = [factor * inverse for factor in factors]
            for h in range(heads):
                columns = slice(h * HD, (h + 1) * HD)
                total = factors[0][:, h : h + 1] * local_out[rows, columns]
                for p in range(1, pages):
                    term = out_in[p - 1, rows, columns].astype(F32)
                    total = total + factors[p][:, h : h + 1] * term
                attention[here, columns] = total.astype(BF16)

        if j == n_tp - 1:
            for other in range(n_tp - 1):
                send_proj(other).wait_recv()
        tile_width = min(features, 1024)

        @pl.loop(0, features // tile_width)
        def _(t):
            columns = pl.ds(pl.multiple_of(t * tile_width, tile_width), tile_width)
            projected = dot(attention[...], w[:, columns]).astype(BF16)
            if j < n_tp - 1:
                proj_send[j, :, columns] = projected
            else:
                summed = projected.astype(F32)
                for other in range(n_tp - 1):
                    summed = summed + proj_in[other, :, columns].astype(F32)
                hidden_ref[:, columns] = (residual[:, columns].astype(F32) + summed).astype(BF16)

        if j < n_tp - 1:
            send_proj(j).start()

    for p in range(1, pages):
        send_lens(p).wait_send()

    @pl.loop(0, chunks)
    def _(c):
        for p in range(1, pages):
            send_q(p, c).wait_send()
            send_lse(p, c).wait_send()
            send_out(p, c).wait_send()

    for j in range(n_tp - 1):
        send_proj(j).wait_send()


def norm_kernel(hidden_ref, gain_ref, path_ref, hidden_out, normed_out, path_out):
    hidden = hidden_ref[...]
    hidden_out[...] = hidden
    wide = hidden.astype(F32)
    mean = jnp.sum(wide * wide, axis=1, keepdims=True) * (1.0 / wide.shape[1])
    normed_out[...] = (wide * lax.rsqrt(mean + 1e-05) * gain_ref[...]).astype(BF16)
    path_out[...] = path_ref[...]


def per_device(n_req, n_tp, queries, new_kv, kv_pool, cache_lens, parents, accepted, residual, w_out, norm_gain):
    requests, pages, page, row_width = kv_pool.shape
    tokens, width = queries.shape
    features = w_out.shape[1]
    part = tokens // n_tp
    chunk = TREE
    chunks = tokens // chunk
    away = pages - 1
    vmem = pl.BlockSpec(memory_space=pltpu.VMEM)
    smem = pl.BlockSpec(memory_space=pltpu.SMEM)
    hbm = pl.BlockSpec(memory_space=pl.ANY)
    dma = pltpu.SemaphoreType.DMA
    hidden, path = pl.pallas_call(
        functools.partial(kernel, n_req, n_tp, chunk),
        out_shape=(
            jax.ShapeDtypeStruct((part, features), BF16),
            jax.ShapeDtypeStruct((requests * PATH, row_width), BF16),
        ),
        in_specs=[smem, smem, vmem, hbm, hbm, hbm, hbm, hbm],
        out_specs=(vmem, vmem),
        scratch_shapes=[
            pltpu.VMEM(queries.shape, BF16),
            pltpu.VMEM(new_kv.shape, BF16),
            pltpu.VMEM((pages, requests, page, row_width), BF16),
            pltpu.VMEM(w_out.shape, BF16),
            pltpu.VMEM((part, features), BF16),
            pltpu.VMEM((away, tokens, width), BF16),
            pltpu.VMEM((requests, LANES), jnp.int32),
            pltpu.VMEM((away, requests, LANES), jnp.int32),
            pltpu.VMEM((away, tokens, width), BF16),
            pltpu.VMEM((away, tokens, width), BF16),
            pltpu.VMEM((away, chunks, 8, LANES), F32),
            pltpu.VMEM((away, chunks, 8, LANES), F32),
            pltpu.VMEM((tokens, width), F32),
            pltpu.VMEM((tokens, LANES), F32),
            pltpu.VMEM((tokens, TREE), F32),
            pltpu.VMEM((part, width), BF16),
            pltpu.VMEM((max(n_tp - 1, 1), part, features), BF16),
            pltpu.VMEM((max(n_tp - 1, 1), part, features), BF16),
            dma((pages + 4,)),
            dma((away,)),
            dma((away,)),
            dma((away, chunks)),
            dma((away, chunks)),
            dma((away, chunks)),
            dma((away, chunks)),
            dma((away, chunks)),
            dma((away, chunks)),
            dma((max(n_tp - 1, 1),)),
            dma((max(n_tp - 1, 1),)),
        ],
        compiler_params=pltpu.CompilerParams(
            collective_id=0, has_side_effects=True, vmem_limit_bytes=56 * 2**20
        ),
    )(cache_lens, accepted, parents, queries, new_kv, kv_pool, residual, w_out)
    rows = 16
    row_block = pl.BlockSpec((rows, features), lambda i: (i, 0))
    whole_path = pl.BlockSpec(path.shape, lambda i: (0, 0))
    hidden_out, normed, path = pl.pallas_call(
        norm_kernel,
        grid=(part // rows,),
        out_shape=(
            jax.ShapeDtypeStruct(hidden.shape, BF16),
            jax.ShapeDtypeStruct(hidden.shape, BF16),
            jax.ShapeDtypeStruct(path.shape, BF16),
        ),
        in_specs=[row_block, pl.BlockSpec((1, features), lambda i: (0, 0)), whole_path],
        out_specs=(row_block, row_block, whole_path),
    )(hidden, norm_gain.reshape(1, features), path)
    return hidden_out, normed, path.reshape(requests, PATH, row_width)


def solution(mesh):
    placed = (
        P("req", "tp"),
        P("req", "tp"),
        P("req", None, None, "tp"),
        P("req"),
        P("req", None),
        P("req"),
        P(("req", "tp"), None),
        P("tp", None),
        P(),
    )
    return jax.shard_map(
        functools.partial(per_device, mesh.shape["req"], mesh.shape["tp"]),
        mesh=mesh,
        in_specs=placed,
        out_specs=(P(("req", "tp"), None), P(("req", "tp"), None), P("req", None, "tp")),
        check_vma=False,
    )
```

```python
import functools

import jax
import jax.numpy as jnp
from jax import lax
from jax.experimental import pallas as pl
from jax.experimental.pallas import tpu as pltpu
from jax.sharding import PartitionSpec as P

HD = 128
TREE = 32
PATH = 8
LANES = 128
NEGATIVE = -1e30
FLOOR = -1e29
SCALE2 = HD**-0.5 * 1.4426950408889634
MESH = pl.DeviceIdType.MESH
F32 = jnp.float32
BF16 = jnp.bfloat16


def iota(shape, axis):
    return lax.broadcasted_iota(jnp.int32, shape, axis)


def dot(left, right):
    return jnp.dot(left, right, preferred_element_type=F32)


def dot_t(left, right):
    return lax.dot_general(left, right, (((1,), (1,)), ((), ())), preferred_element_type=F32)


def indicator(mask, dtype=BF16):
    return jnp.where(mask, 1.0, 0.0).astype(dtype)


def tree_masks(parents, tokens):
    requests = tokens // TREE
    expand = indicator((iota((tokens, requests), 0) >> 5) == iota((tokens, requests), 1), F32)
    spread = dot(expand, parents.astype(F32))
    pick = (iota((tokens, TREE), 0) & (TREE - 1)) == iota((tokens, TREE), 1)
    parent = jnp.sum(jnp.where(pick, spread, 0.0), axis=1, keepdims=True)
    rows, columns = iota((tokens, tokens), 0), iota((tokens, tokens), 1)
    base = (rows & ~(TREE - 1)).astype(F32)
    one = indicator(columns.astype(F32) == parent + base, F32)
    eye = indicator(rows == columns, F32)
    two = dot(one.astype(BF16), one.astype(BF16))
    four = dot(two.astype(BF16), two.astype(BF16))
    reach = dot((eye + one).astype(BF16), (eye + two).astype(BF16))
    reach = dot(reach.astype(BF16), (eye + four).astype(BF16))
    return indicator(reach > 0.0)


def kernel(
    n_req, n_tp, chunk,
    lens_s, accepted_s, parents_ref, q_hbm, fresh_hbm, kv_hbm, residual_hbm, w_hbm,
    hidden_ref, path_ref,
    q_ref, fresh_ref, kv, w, residual, q_in, lens_own, lens_in, out_send, out_in, lse_send, lse_in,
    local_out, local_lse, tree, attention, proj_send, proj_in,
    load_sem, lens_send_sem, lens_recv_sem, q_send_sem, q_recv_sem, o_send_sem, o_recv_sem,
    l_send_sem, l_recv_sem, p_send_sem, p_recv_sem, f_send_sem,
):
    me, tp = lax.axis_index("req"), lax.axis_index("tp")
    tokens, width = q_ref.shape
    requests = tokens // TREE
    heads = width // HD
    kv_heads = fresh_ref.shape[1] // (2 * HD)
    pages, page = kv.shape[0], kv.shape[2]
    part = tokens // n_tp
    per_part = part // chunk
    chunks = tokens // chunk
    features = w.shape[1]
    group = heads // kv_heads

    first_loads = [
        pltpu.make_async_copy(fresh_hbm, fresh_ref, load_sem.at[pages + 2]),
        pltpu.make_async_copy(q_hbm, q_ref, load_sem.at[pages + 3]),
    ]
    loads = [
        pltpu.make_async_copy(kv_hbm.at[:, p], kv.at[p], load_sem.at[p]) for p in range(pages)
    ]
    loads.append(pltpu.make_async_copy(w_hbm, w, load_sem.at[pages]))
    loads.append(pltpu.make_async_copy(residual_hbm, residual, load_sem.at[pages + 1]))
    for load in first_loads + loads:
        load.start()

    def ahead(p):
        return lax.rem(me + p, n_req)

    def behind(p):
        return lax.rem(me + n_req - p, n_req)

    barrier = pltpu.get_barrier_semaphore()
    for p in range(1, pages):
        for other in (ahead(p), behind(p)):
            pl.semaphore_signal(barrier, inc=1, device_id={"req": other}, device_id_type=MESH)
    for j in range(1, n_tp):
        pl.semaphore_signal(
            barrier, inc=1, device_id={"tp": lax.rem(tp + j, n_tp)}, device_id_type=MESH
        )

    lens = jnp.zeros((requests, LANES), jnp.int32)
    for r in range(requests):
        lens = jnp.where(iota((requests, LANES), 0) == r, lens_s[r], lens)
    lens_own[...] = lens
    pl.semaphore_wait(barrier, 2 * (pages - 1) + n_tp - 1)

    def first_row(c):
        block = lax.rem(tp + 1 + c // per_part, n_tp)
        return pl.multiple_of(block * part + lax.rem(c, per_part) * chunk, chunk)

    def send_lens(p):
        return pltpu.make_async_remote_copy(
            lens_own, lens_in.at[p - 1], lens_send_sem.at[p - 1], lens_recv_sem.at[p - 1],
            device_id={"req": ahead(p)}, device_id_type=MESH,
        )

    def send_q(p, c):
        rows = pl.ds(first_row(c), chunk)
        return pltpu.make_async_remote_copy(
            q_hbm.at[rows], q_in.at[p - 1, rows], q_send_sem.at[p - 1, c], q_recv_sem.at[p - 1, c],
            device_id={"req": ahead(p)}, device_id_type=MESH,
        )

    def send_out(p, c):
        rows = pl.ds(first_row(c), chunk)
        return pltpu.make_async_remote_copy(
            out_send.at[p - 1, rows], out_in.at[p - 1, rows],
            o_send_sem.at[p - 1, c], o_recv_sem.at[p - 1, c],
            device_id={"req": behind(p)}, device_id_type=MESH,
        )

    def send_lse(p, c):
        return pltpu.make_async_remote_copy(
            lse_send.at[p - 1, c], lse_in.at[p - 1, c],
            l_send_sem.at[p - 1, c], l_recv_sem.at[p - 1, c],
            device_id={"req": behind(p)}, device_id_type=MESH,
        )

    def send_proj(j):
        return pltpu.make_async_remote_copy(
            proj_send.at[j], proj_in.at[j], p_send_sem.at[j], p_recv_sem.at[j],
            device_id={"tp": lax.rem(tp + 1 + j, n_tp)}, device_id_type=MESH,
        )

    for p in range(1, pages):
        send_lens(p).start()

    odd = lax.rem(me, 2)
    direct = (1 + 2 * odd, 2)

    @pl.loop(0, chunks)
    def _(c):
        for p in direct:
            send_q(p, c).start()

    def passed(c):
        even_turn = 1 - lax.rem(c, 2)
        return 2 * (1 - even_turn) + even_turn * (3 - 2 * odd)

    def forward(c):
        even_turn = 1 - lax.rem(c, 2)
        source = passed(c)
        target = even_turn * (1 + 2 * odd) + (1 - even_turn) * (3 - 2 * odd)
        step = even_turn * (4 * odd - 2) + (1 - even_turn) * (1 - 2 * odd)
        rows = pl.ds(first_row(c), chunk)
        return pltpu.make_async_remote_copy(
            q_in.at[source - 1, rows], q_in.at[target - 1, rows],
            f_send_sem.at[c], q_recv_sem.at[target - 1, c],
            device_id={"req": lax.rem(me + n_req + step, n_req)}, device_id_type=MESH,
        )

    def pass_on(c):
        send_q(passed(c), c).wait_recv()
        forward(c).start()

    marked = tree_masks(parents_ref[...], tokens)
    fold = indicator((iota((tokens, TREE), 0) & (TREE - 1)) == iota((tokens, TREE), 1))
    tree[...] = dot(marked, fold)
    accepted = jnp.zeros((requests, tokens), jnp.int32)
    for r in range(requests):
        accepted = jnp.where(iota((requests, tokens), 0) == r, accepted_s[r] + r * TREE, accepted)
    chosen = indicator(iota((requests, tokens), 1) == accepted, F32)
    on_path = dot(chosen, marked.astype(F32))
    upto = indicator(iota((tokens, tokens), 0) <= iota((tokens, tokens), 1), F32)
    count = dot(on_path, upto)
    slots = (requests * PATH, requests)
    spread = indicator((iota(slots, 0) >> 3) == iota(slots, 1), F32)
    slot = (iota((requests * PATH, tokens), 0) & (PATH - 1)).astype(F32) + 1.0
    selector = (dot(spread, count) == slot) & (dot(spread, on_path) > 0.0)
    first_loads[0].wait()
    path_ref[...] = dot(indicator(selector), fresh_ref[...]).astype(BF16)

    lane = iota((TREE, LANES), 1)

    def stacked_queries(ref, rows, k):
        columns = [slice((k * group + g) * HD, (k * group + g + 1) * HD) for g in range(group)]
        return jnp.concatenate([ref[rows, c] for c in columns], axis=0)

    def lens_mask(row, p):
        wide = jnp.concatenate([row] * (page // LANES), axis=1)
        return iota((1, page), 1) + p * page < wide

    ones = jnp.ones((page, HD), BF16)
    units = [(i, k) for i in range(chunk // TREE) for k in range(kv_heads)]

    def key_columns(k):
        return slice(2 * k * HD, (2 * k + 1) * HD)

    def value_columns(k):
        return slice((2 * k + 1) * HD, (2 * k + 2) * HD)

    def with_ones(value_rows):
        return jnp.concatenate([value_rows, ones[: value_rows.shape[0]]], axis=1)

    def by_token(levels, i):
        lse = jnp.zeros((TREE, LANES), F32)
        for k in range(kv_heads):
            for g in range(group):
                level = levels[i * kv_heads + k][g * TREE : (g + 1) * TREE]
                lse = jnp.where(lane == k * group + g, level, lse)
        return lse

    def token_rows(start, i):
        return pl.ds(pl.multiple_of(start + i * TREE, TREE), TREE)

    def local_chunk(start):
        first = start // TREE
        valid = [lens_mask(lens_own[pl.ds(first + i, 1), :], 0) for i in range(chunk // TREE)]
        allowed = [
            jnp.concatenate([tree[token_rows(start, i), :]] * group, axis=0) > 0.0
            for i in range(chunk // TREE)
        ]
        queries = [stacked_queries(q_ref, token_rows(start, i), k) for i, k in units]
        cached = [
            jnp.where(valid[i], dot_t(query, kv[0, first + i, :, key_columns(k)]) * SCALE2, NEGATIVE)
            for query, (i, k) in zip(queries, units)
        ]
        drafted = [
            jnp.where(
                allowed[i],
                dot_t(query, fresh_ref[token_rows(start, i), key_columns(k)]) * SCALE2,
                NEGATIVE,
            )
            for query, (i, k) in zip(queries, units)
        ]
        largest = [
            jnp.maximum(jnp.max(old, axis=1, keepdims=True), jnp.max(new, axis=1, keepdims=True))
            for old, new in zip(cached, drafted)
        ]
        cached = [jnp.exp2(old - top).astype(BF16) for old, top in zip(cached, largest)]
        drafted = [jnp.exp2(new - top).astype(BF16) for new, top in zip(drafted, largest)]
        sums = [
            dot(old, with_ones(kv[0, first + i, :, value_columns(k)]))
            + dot(new, with_ones(fresh_ref[token_rows(start, i), value_columns(k)]))
            for old, new, (i, k) in zip(cached, drafted, units)
        ]
        levels = []
        for both, top, (i, k) in zip(sums, largest, units):
            total = both[:, HD:]
            out = both[:, :HD] / total
            levels.append(top + jnp.log2(total))
            for g in range(group):
                h = k * group + g
                local_out[token_rows(start, i), h * HD : (h + 1) * HD] = out[g * TREE : (g + 1) * TREE]
        for i in range(chunk // TREE):
            local_lse[token_rows(start, i), :] = by_token(levels, i)

    away = [(p, i, k) for p in range(1, pages) for i, k in units]

    def remote_chunk(start, c):
        first = start // TREE
        valid = {
            (p, i): lens_mask(lens_in[p - 1, pl.ds(first + i, 1), :], p)
            for p in range(1, pages)
            for i in range(chunk // TREE)
        }
        cached = [
            jnp.where(
                valid[p, i],
                dot_t(
                    stacked_queries(q_in.at[p - 1], token_rows(start, i), k),
                    kv[p, first + i, :, key_columns(k)],
                )
                * SCALE2,
                NEGATIVE,
            )
            for p, i, k in away
        ]
        largest = [jnp.max(scores, axis=1, keepdims=True) for scores in cached]
        cached = [
            jnp.exp2(scores - jnp.maximum(top, FLOOR)).astype(BF16)
            for scores, top in zip(cached, largest)
        ]
        sums = [
            dot(weights, with_ones(kv[p, first + i, :, value_columns(k)]))
            for weights, (p, i, k) in zip(cached, away)
        ]
        levels = []
        for both, top, (p, i, k) in zip(sums, largest, away):
            total = jnp.maximum(both[:, HD:], 1.0)
            out = (both[:, :HD] / total).astype(BF16)
            levels.append(top + jnp.log2(total))
            for g in range(group):
                h = k * group + g
                out_send[p - 1, token_rows(start, i), h * HD : (h + 1) * HD] = out[
                    g * TREE : (g + 1) * TREE
                ]
        for p in range(1, pages):
            some = levels[(p - 1) * len(units) : p * len(units)]
            rows = [by_token(some, i) for i in range(chunk // TREE)]
            rows.append(jnp.zeros((LANES - chunk, LANES), F32))
            lse_send[p - 1, c] = jnp.concatenate(rows, axis=0).T[:8]

    pass_on(0)
    first_loads[1].wait()
    loads[0].wait()
    local_chunk(first_row(0))
    for p in range(1, pages):
        loads[p].wait()
        send_lens(p).wait_recv()

    @pl.loop(0, chunks)
    def _(c):
        @pl.when(c < chunks - 1)
        def _():
            pass_on(c + 1)

        for turn in range(1, pages - 1):
            send_q(1 + lax.rem(passed(c) - 1 + turn, pages - 1), c).wait_recv()
        remote_chunk(first_row(c), c)
        for p in range(1, pages):
            send_lse(p, c).start()
            send_out(p, c).start()

        @pl.when(c < chunks - 1)
        def _():
            local_chunk(first_row(c + 1))

    loads[pages].wait()
    loads[pages + 1].wait()

    for j in range(n_tp):

        @pl.loop(0, per_part)
        def _(i):
            c = j * per_part + i
            rows = pl.ds(first_row(c), chunk)
            here = pl.ds(pl.multiple_of(i * chunk, chunk), chunk)
            levels = [local_lse[rows, :]]
            for p in range(1, pages):
                send_lse(p, c).wait_recv()
                send_out(p, c).wait_recv()
                tile = jnp.concatenate(
                    [lse_in[p - 1, c], jnp.zeros((LANES - 8, LANES), F32)], axis=0
                )
                levels.append(tile.T[:chunk])
            largest = functools.reduce(jnp.maximum, levels)
            factors = [jnp.exp2(level - largest) for level in levels]
            inverse = 1.0 / functools.reduce(jnp.add, factors)
            factors = [factor * inverse for factor in factors]
            for h in range(heads):
                columns = slice(h * HD, (h + 1) * HD)
                total = factors[0][:, h : h + 1] * local_out[rows, columns]
                for p in range(1, pages):
                    term = out_in[p - 1, rows, columns].astype(F32)
                    total = total + factors[p][:, h : h + 1] * term
                attention[here, columns] = total.astype(BF16)

        if j == n_tp - 1:
            for other in range(n_tp - 1):
                send_proj(other).wait_recv()
        tile_width = min(features, 1024)

        @pl.loop(0, features // tile_width)
        def _(t):
            columns = pl.ds(pl.multiple_of(t * tile_width, tile_width), tile_width)
            projected = dot(attention[...], w[:, columns]).astype(BF16)
            if j < n_tp - 1:
                proj_send[j, :, columns] = projected
            else:
                summed = projected.astype(F32)
                for other in range(n_tp - 1):
                    summed = summed + proj_in[other, :, columns].astype(F32)
                hidden_ref[:, columns] = (residual[:, columns].astype(F32) + summed).astype(BF16)

        if j < n_tp - 1:
            send_proj(j).start()

    for p in range(1, pages):
        send_lens(p).wait_send()

    @pl.loop(0, chunks)
    def _(c):
        forward(c).wait_send()
        for p in direct:
            send_q(p, c).wait_send()
        for p in range(1, pages):
            send_lse(p, c).wait_send()
            send_out(p, c).wait_send()

    for j in range(n_tp - 1):
        send_proj(j).wait_send()


def norm_kernel(hidden_ref, gain_ref, path_ref, hidden_out, normed_out, path_out):
    hidden = hidden_ref[...]
    hidden_out[...] = hidden
    wide = hidden.astype(F32)
    mean = jnp.sum(wide * wide, axis=1, keepdims=True) * (1.0 / wide.shape[1])
    normed_out[...] = (wide * lax.rsqrt(mean + 1e-05) * gain_ref[...]).astype(BF16)
    path_out[...] = path_ref[...]


def per_device(n_req, n_tp, queries, new_kv, kv_pool, cache_lens, parents, accepted, residual, w_out, norm_gain):
    requests, pages, page, row_width = kv_pool.shape
    tokens, width = queries.shape
    features = w_out.shape[1]
    part = tokens // n_tp
    chunk = TREE
    chunks = tokens // chunk
    away = pages - 1
    vmem = pl.BlockSpec(memory_space=pltpu.VMEM)
    smem = pl.BlockSpec(memory_space=pltpu.SMEM)
    hbm = pl.BlockSpec(memory_space=pl.ANY)
    dma = pltpu.SemaphoreType.DMA
    hidden, path = pl.pallas_call(
        functools.partial(kernel, n_req, n_tp, chunk),
        out_shape=(
            jax.ShapeDtypeStruct((part, features), BF16),
            jax.ShapeDtypeStruct((requests * PATH, row_width), BF16),
        ),
        in_specs=[smem, smem, vmem, hbm, hbm, hbm, hbm, hbm],
        out_specs=(vmem, vmem),
        scratch_shapes=[
            pltpu.VMEM(queries.shape, BF16),
            pltpu.VMEM(new_kv.shape, BF16),
            pltpu.VMEM((pages, requests, page, row_width), BF16),
            pltpu.VMEM(w_out.shape, BF16),
            pltpu.VMEM((part, features), BF16),
            pltpu.VMEM((away, tokens, width), BF16),
            pltpu.VMEM((requests, LANES), jnp.int32),
            pltpu.VMEM((away, requests, LANES), jnp.int32),
            pltpu.VMEM((away, tokens, width), BF16),
            pltpu.VMEM((away, tokens, width), BF16),
            pltpu.VMEM((away, chunks, 8, LANES), F32),
            pltpu.VMEM((away, chunks, 8, LANES), F32),
            pltpu.VMEM((tokens, width), F32),
            pltpu.VMEM((tokens, LANES), F32),
            pltpu.VMEM((tokens, TREE), F32),
            pltpu.VMEM((part, width), BF16),
            pltpu.VMEM((max(n_tp - 1, 1), part, features), BF16),
            pltpu.VMEM((max(n_tp - 1, 1), part, features), BF16),
            dma((pages + 4,)),
            dma((away,)),
            dma((away,)),
            dma((away, chunks)),
            dma((away, chunks)),
            dma((away, chunks)),
            dma((away, chunks)),
            dma((away, chunks)),
            dma((away, chunks)),
            dma((max(n_tp - 1, 1),)),
            dma((max(n_tp - 1, 1),)),
            dma((chunks,)),
        ],
        compiler_params=pltpu.CompilerParams(
            collective_id=0, has_side_effects=True, vmem_limit_bytes=56 * 2**20
        ),
    )(cache_lens, accepted, parents, queries, new_kv, kv_pool, residual, w_out)
    rows = min(part, 2 * TREE)
    row_block = pl.BlockSpec((rows, features), lambda i: (i, 0))
    whole_path = pl.BlockSpec(path.shape, lambda i: (0, 0))
    hidden_out, normed, path = pl.pallas_call(
        norm_kernel,
        grid=(part // rows,),
        out_shape=(
            jax.ShapeDtypeStruct(hidden.shape, BF16),
            jax.ShapeDtypeStruct(hidden.shape, BF16),
            jax.ShapeDtypeStruct(path.shape, BF16),
        ),
        in_specs=[row_block, pl.BlockSpec((1, features), lambda i: (0, 0)), whole_path],
        out_specs=(row_block, row_block, whole_path),
    )(hidden, norm_gain.reshape(1, features), path)
    return hidden_out, normed, path.reshape(requests, PATH, row_width)


def solution(mesh):
    placed = (
        P("req", "tp"),
        P("req", "tp"),
        P("req", None, None, "tp"),
        P("req"),
        P("req", None),
        P("req"),
        P(("req", "tp"), None),
        P("tp", None),
        P(),
    )
    return jax.shard_map(
        functools.partial(per_device, mesh.shape["req"], mesh.shape["tp"]),
        mesh=mesh,
        in_specs=placed,
        out_specs=(P(("req", "tp"), None), P(("req", "tp"), None), P("req", None, "tp")),
        check_vma=False,
    )
```
